32 devices in a mesh: tm: 4 (over z), height: 4 (over y, x), width: 2 (over core).
Axes of the slice: x: 2, y: 2, z: 4, core: 2. Of those that a mesh axis runs over, the one named last changes fastest.
Arguments:
- video: bfloat16 [2, 128, 8, 256, 128], P('width', ('tm', 'height')), may hold values from -6 to 6
- out_grad: bfloat16 [2, 128, 8, 256, 128], P('width', None, 'tm', 'height'), may hold values from -6 to 6
- lengths: int32 [4], replicated, may hold values from 1 to 3, 8 in all
- temporal_weight: bfloat16 [3, 128, 128], replicated, may hold values from -0.3125 to 0.3125
- spatial_weight: bfloat16 [3, 3, 128, 128], replicated, may hold values from -0.1875 to 0.1875
Outputs:
- video_grad: bfloat16 [2, 128, 8, 256, 128], P('width', ('tm', 'height'))
- temporal_grad: float32 [3, 128, 128], replicated
- spatial_grad: float32 [3, 3, 128, 128], replicated
The draws below stay inside these ranges and needn't reach their ends.
Inputs may be any that keep to these rules, and one draw needn't show every extreme that they name: The 4 clips lie end to end in frame order, their lengths sum to 8, and the longest clip has exactly 3 frames.
All inputs are finite; a program needn't handle non-finite values.
Results may differ from the reference program's by a relative error of at most 0.008.
Values may be sent and summed in bfloat16 or wider, within the bound.
No kernel may reach another device: no remote copies, remote signals or barrier semaphores. Data moves between devices by JAX's collectives and lax.ppermute only.
A program may use at most 192 MiB of HBM per device.

```python
import math
import jax
import jax.numpy as jnp
import numpy as np
from jax import lax

C = 128
NCLIP = 4
H = 256
F = 8
WL = 128
N_WIDTH = 2


def steps_of(stream_key, extent, split, smallest, largest):
    factor_of = 1.0
    for dim, parts in split:
        steps = jax.random.uniform(jax.random.fold_in(jax.random.fold_in(stream_key, 6), dim), (parts,), jnp.float32, smallest / len(split), largest / len(split))
        factor_of = factor_of * jnp.repeat(jnp.exp(steps), extent[dim] // parts).reshape((-1,) + (1,) * (len(extent) - 1 - dim))
    return factor_of


def length_profile(number_of, total, most, skew):
    loads = [(1 << 20) // math.isqrt(standing ** skew) + 1 for standing in range(2, number_of + 1)]
    rest, counts = total - most - (number_of - 1), [1] * (number_of - 1)
    while rest > 0:
        movable = [i for i in range(number_of - 1) if counts[i] < most]
        mass, budget = sum([loads[i] for i in movable]), rest
        for i in movable:
            extra = min(most - counts[i], max(1, budget * loads[i] // mass), rest)
            counts[i] = counts[i] + extra
            rest = rest - extra
    return np.array([most] + counts)


def ragged(key, number_of, total, reach, lean):
    if number_of == 2:
        one = jax.random.randint(key, (), max(1, total - reach), min(reach, total - 1) + 1)
        return jnp.stack([one, total - one])
    sizes = jnp.asarray(length_profile(number_of, total, reach, lean), jnp.int32)
    couples = (number_of - 1) // 2
    donor, sink = sizes[1:1 + 2 * couples:2], sizes[2:2 + 2 * couples:2]
    room = jnp.minimum(donor - 1, reach - sink)
    shifted = jax.random.randint(jax.random.fold_in(key, 1), (couples,), 0, 1 << 20) % (room + 1)
    sizes = sizes.at[1:1 + 2 * couples:2].set(donor - shifted).at[2:2 + 2 * couples:2].set(sink + shifted)
    return sizes[jax.random.permutation(jax.random.fold_in(key, 2), number_of)]


def centred(own_key, dims, width, most, cuts=(), kind=jnp.bfloat16):
    array = jax.random.normal(own_key, dims, jnp.float32) * width
    if len(cuts) > 0:
        array = steps_of(own_key, dims, cuts, -0.22, 0.18) * array
    return jnp.clip(array, min=-most, max=most).astype(kind)


def setup_inputs(seed: int = 0) -> dict:
    key_of = jax.random.split(jax.random.key(seed), 6)
    return {
        "video": centred(key_of[0], (N_WIDTH, WL, F, H, C), 1.0, 6.0, ((0, 2), (1, 16))),
        "out_grad": centred(key_of[1], (N_WIDTH, WL, F, H, C), 1.0, 6.0, ((0, 2), (2, 4), (3, 4))),
        "lengths": ragged(key_of[2], NCLIP, F, F // 3 + 1, 2).astype(jnp.int32),
        "temporal_weight": centred(key_of[3], (3, C, C), (3 * C) ** -0.5, 0.3125),
        "spatial_weight": centred(key_of[4], (3, 3, C, C), (9 * C) ** -0.5, 0.1875),
    }


def frame_masks(lengths, frames):
    ends = jnp.cumsum(lengths, dtype=jnp.int32)
    starts = ends - lengths
    frame_index = jnp.arange(frames, dtype=jnp.int32)
    inside = (frame_index[:, None] >= starts[None, :]) & (frame_index[:, None] < ends[None, :])
    first = jnp.sum(jnp.where(inside, starts[None, :], 0), axis=1, dtype=jnp.int32)
    return jnp.stack([(frame_index - lag >= first) for lag in range(3)]).astype(jnp.bfloat16)


def silu_slope(pre, grads):
    sig = jax.nn.sigmoid(pre)
    return grads.astype(jnp.float32) * sig * (1.0 + pre * (1.0 - sig))


def reference(video, out_grad, lengths, temporal_weight, spatial_weight):
    halves = video.shape[0]
    frames = video.shape[2]
    rows = video.shape[3]
    chans = video.shape[4]
    cols = halves * video.shape[1]
    clip = jnp.transpose(video, (2, 3, 0, 1, 4)).reshape(frames, rows, cols, chans)
    grads = jnp.transpose(out_grad, (2, 3, 0, 1, 4)).reshape(frames, rows, cols, chans)
    masks = frame_masks(lengths, frames)
    padded = jnp.pad(clip, ((2, 0), (0, 0), (0, 0), (0, 0)))
    frame_ids = jnp.arange(frames, dtype=jnp.int32)

    def tap(frame, lag):
        piece = lax.dynamic_index_in_dim(padded, frame + 2 - lag, 0, keepdims=False)
        weight = lax.dynamic_index_in_dim(masks[lag], frame, 0, keepdims=False)
        return (piece * weight).reshape(-1, chans)

    def forward_frame(frame):
        total = jnp.zeros((rows * cols, chans), jnp.float32)
        for lag in range(3):
            total = total + jnp.dot(tap(frame, lag), temporal_weight[lag], preferred_element_type=jnp.float32)
        return total.astype(jnp.bfloat16).reshape(rows, cols, chans)

    act = lax.map(forward_frame, frame_ids)

    def spatial_step(accum, inputs):
        act_frame, grad_frame = inputs
        padded_act = jnp.pad(act_frame, ((1, 1), (1, 1), (0, 0)))
        pre = jnp.zeros((rows * cols, chans), jnp.float32)
        for row_off in range(3):
            for col_off in range(3):
                piece = padded_act[row_off:row_off + rows, col_off:col_off + cols].reshape(-1, chans)
                pre = pre + jnp.dot(piece, spatial_weight[row_off, col_off], preferred_element_type=jnp.float32)
        delta = silu_slope(pre, grad_frame.reshape(-1, chans)).astype(jnp.bfloat16)
        padded_delta = jnp.pad(delta.reshape(rows, cols, chans), ((1, 1), (1, 1), (0, 0)))
        back = jnp.zeros((rows * cols, chans), jnp.float32)
        terms = []
        for row_off in range(3):
            line = []
            for col_off in range(3):
                piece = padded_delta[2 - row_off:2 - row_off + rows, 2 - col_off:2 - col_off + cols].reshape(-1, chans)
                back = back + jnp.dot(piece, spatial_weight[row_off, col_off].T, preferred_element_type=jnp.float32)
                source = padded_act[row_off:row_off + rows, col_off:col_off + cols].reshape(-1, chans)
                line.append(lax.dot_general(source, delta, (((0,), (0,)), ((), ())), preferred_element_type=jnp.float32))
            terms.append(jnp.stack(line))
        return accum + jnp.stack(terms), back.astype(jnp.bfloat16).reshape(rows, cols, chans)

    spatial_sum, act_grad = lax.scan(spatial_step, jnp.zeros((3, 3, chans, chans), jnp.float32), (act, grads))
    padded_grad = jnp.pad(act_grad, ((0, 2), (0, 0), (0, 0), (0, 0)))
    padded_mask = jnp.pad(masks, ((0, 0), (0, 2)))

    def backward_step(accum, frame):
        total = jnp.zeros((rows * cols, chans), jnp.float32)
        current = lax.dynamic_index_in_dim(act_grad, frame, 0, keepdims=False).reshape(-1, chans)
        terms = []
        for lag in range(3):
            later = lax.dynamic_index_in_dim(padded_grad, frame + lag, 0, keepdims=False)
            weight = lax.dynamic_index_in_dim(padded_mask[lag], frame + lag, 0, keepdims=False)
            total = total + jnp.dot((later * weight).reshape(-1, chans), temporal_weight[lag].T, preferred_element_type=jnp.float32)
            terms.append(lax.dot_general(tap(frame, lag), current, (((0,), (0,)), ((), ())), preferred_element_type=jnp.float32))
        return accum + jnp.stack(terms), total.astype(jnp.bfloat16).reshape(rows, cols, chans)

    temporal_sum, frame_grad = lax.scan(backward_step, jnp.zeros((3, chans, chans), jnp.float32), frame_ids)
    video_grad = jnp.transpose(frame_grad.reshape(frames, rows, halves, cols // halves, chans), (2, 3, 0, 1, 4))
    scale = float(frames * rows * cols) ** -0.5
    return video_grad, temporal_sum * scale, spatial_sum * scale
```

```python
import functools

import jax
import jax.numpy as jnp
from jax import lax
from jax.experimental import pallas as pl
from jax.experimental.pallas import tpu as pltpu
from jax.sharding import PartitionSpec as P

MESH_AXES = ("tm", "height", "width")
VMEM = 40 * 1024 * 1024


def frame_masks(lengths, frames):
    ends = jnp.cumsum(lengths, dtype=jnp.int32)
    starts = ends - lengths
    frame_index = jnp.arange(frames, dtype=jnp.int32)
    inside = (frame_index[:, None] >= starts[None, :]) & (frame_index[:, None] < ends[None, :])
    first = jnp.sum(jnp.where(inside, starts[None, :], 0), axis=1, dtype=jnp.int32)
    return jnp.stack([frame_index - lag >= first for lag in range(3)]).astype(jnp.bfloat16)


def column_neighbours(first, last):
    n_tm, n_height, n_width = (lax.axis_size(axis) for axis in MESH_AXES)
    blocks = n_tm * n_height
    place = [(pos % blocks) * n_width + pos // blocks for pos in range(blocks * n_width)]
    pairs = list(zip(place[:-1], place[1:]))
    left = lax.ppermute(last, MESH_AXES, pairs)
    right = lax.ppermute(first, MESH_AXES, [(b, a) for a, b in pairs])
    return left, right


def block_table(rows, cols, entry):
    blocks = [[entry(i, j) for j in range(cols)] for i in range(rows)]
    some = next(b for line in blocks for b in line if b is not None)
    zero = jnp.zeros_like(some)
    return jnp.concatenate(
        [jnp.concatenate([zero if b is None else b for b in line], axis=-1) for line in blocks],
        axis=-2,
    )


def row_shifts(block, rows):
    index = lax.broadcasted_iota(jnp.int32, block.shape, 0)
    above = jnp.where(index == 0, 0.0, pltpu.roll(block, 1, 0))
    below = jnp.where(index == rows - 1, 0.0, pltpu.roll(block, rows - 1, 0))
    return above.astype(jnp.bfloat16), below.astype(jnp.bfloat16)


def lanes(parts):
    return parts[0] if len(parts) == 1 else jnp.concatenate(parts, axis=1)


def forward_kernel(group, width, lag, *refs):
    now, before = refs[:group], refs[group : 2 * group]
    left, left_before, right, right_before, temporal, spatial, slope, cube, held = refs[2 * group :]
    step = pl.program_id(1)
    rows, chans = slope.shape[2], slope.shape[3]
    sources = []
    for e in range(group):
        ext = step * group + e
        line = []
        for ours, l_ref, r_ref in ((before[e], left_before, right_before), (now[e], left, right)):
            for frame in range(2):
                tile = ours[0, frame]
                tile = jnp.where(ext == 0, l_ref[0, frame], tile)
                tile = jnp.where(ext == width + 1, r_ref[0, frame], tile)
                line.append(tile)
        sources.append(lanes(line))
    mixed = jnp.dot(
        jnp.concatenate(sources, axis=0), temporal[0], preferred_element_type=jnp.float32
    ).astype(jnp.bfloat16)
    for e in range(group):
        act = mixed[e * rows : (e + 1) * rows]
        above, below = row_shifts(act.astype(jnp.float32), rows)
        for frame in range(2):
            at = slice(frame * chans, (frame + 1) * chans)
            value = lanes([above[:, at], act[:, at], below[:, at]])
            held[step * group + e, frame] = value
            cube[e, frame] = value

    @pl.when(step >= lag)
    def _():
        base = (step - lag) * group
        source = lanes([held[base + k].reshape(2 * rows, 3 * chans) for k in range(group + 2)])
        pre = jnp.dot(source, spatial[...], preferred_element_type=jnp.float32)
        sig = jax.nn.sigmoid(pre)
        value = sig * (1.0 + pre * (1.0 - sig))
        for e in range(group):
            slope[e] = value[:, e * chans : (e + 1) * chans].reshape(2, rows, chans)


def forward(video, left, right, temporal, spatial, group):
    width, frames, rows, chans = video.shape
    lag = 2 // group
    steps = (width + 2) // group

    def own(e, back):
        return pl.BlockSpec(
            (1, 2, rows, chans),
            lambda p, j: (
                jnp.clip(j * group + e - 1, 0, width - 1),
                jnp.maximum(p - back, 0),
                0,
                0,
            ),
        )

    def edge(back):
        return pl.BlockSpec((1, 2, rows, chans), lambda p, j: (0, jnp.maximum(p - back, 0), 0, 0))

    pixels = width * frames * rows
    return pl.pallas_call(
        functools.partial(forward_kernel, group, width, lag),
        grid=(frames // 2, steps),
        in_specs=[own(e, 0) for e in range(group)]
        + [own(e, 1) for e in range(group)]
        + [
            edge(0),
            edge(1),
            edge(0),
            edge(1),
            pl.BlockSpec((1, 4 * chans, 2 * chans), lambda p, j: (p, 0, 0)),
            pl.BlockSpec(spatial.shape, lambda p, j: (0, 0)),
        ],
        out_specs=[
            pl.BlockSpec(
                (group, 2, rows, chans), lambda p, j: (jnp.maximum(j - lag, 0), p, 0, 0)
            ),
            pl.BlockSpec((group, 2, rows, 3 * chans), lambda p, j: (j, p, 0, 0)),
        ],
        out_shape=[
            jax.ShapeDtypeStruct((width, frames, rows, chans), jnp.float32),
            jax.ShapeDtypeStruct((width + 2, frames, rows, 3 * chans), jnp.bfloat16),
        ],
        scratch_shapes=[pltpu.VMEM((width + 2, 2, rows, 3 * chans), jnp.bfloat16)],
        compiler_params=pltpu.CompilerParams(vmem_limit_bytes=VMEM),
        cost_estimate=pl.CostEstimate(
            flops=pixels * chans * chans * 2 * 24,
            bytes_accessed=pixels * chans * 14,
            transcendentals=pixels * chans,
        ),
    )(*([video] * (2 * group)), left, left, right, right, temporal, spatial)


def slope_kernel(group, extra, *refs):
    grads, slope = refs[:2]
    cubes = refs[2 : 2 + extra]
    delta, total = refs[2 + extra :]
    bands, band = grads.shape[1], grads.shape[4]
    rows, chans = slope.shape[2], slope.shape[3]
    for e in range(group):
        for frame in range(2):
            for b in range(bands):
                at = slice(b * band, (b + 1) * band)
                value = grads[0, b, e, frame].astype(jnp.float32) * slope[e, frame, at]
                delta[e, frame, at] = value.astype(jnp.bfloat16)
    first = (pl.program_id(0) == 0) & (pl.program_id(1) == 0)

    @pl.when(first)
    def _():
        total[...] = jnp.zeros_like(total)

    own = lanes([delta[e].reshape(2 * rows, chans) for e in range(group)])
    source = lanes(
        [
            cubes[k // group][k % group].reshape(2 * rows, 3 * chans)
            for k in range(group + 2)
        ]
    )
    total[...] += lax.dot_general(
        own, source, (((0,), (0,)), ((), ())), preferred_element_type=jnp.float32
    )


def slopes(received, slope, cube, group):
    width, frames, rows, chans = slope.shape
    bands, band = received.shape[1], received.shape[4]
    extra = 2 // group + 1
    pixels = width * frames * rows
    return pl.pallas_call(
        functools.partial(slope_kernel, group, extra),
        grid=(frames // 2, width // group),
        in_specs=[
            pl.BlockSpec((1, bands, group, 2, band, chans), lambda p, i: (p, 0, i, 0, 0, 0)),
            pl.BlockSpec((group, 2, rows, chans), lambda p, i: (i, p, 0, 0)),
        ]
        + [
            pl.BlockSpec(
                (group, 2, rows, 3 * chans), functools.partial(lambda k, p, i: (i + k, p, 0, 0), k)
            )
            for k in range(extra)
        ],
        out_specs=[
            pl.BlockSpec((group, 2, rows, chans), lambda p, i: (i, p, 0, 0)),
            pl.BlockSpec((group * chans, (group + 2) * 3 * chans), lambda p, i: (0, 0)),
        ],
        out_shape=[
            jax.ShapeDtypeStruct((width, frames, rows, chans), jnp.bfloat16),
            jax.ShapeDtypeStruct((group * chans, (group + 2) * 3 * chans), jnp.float32),
        ],
        compiler_params=pltpu.CompilerParams(vmem_limit_bytes=VMEM),
        cost_estimate=pl.CostEstimate(
            flops=pixels * chans * chans * 2 * 18,
            bytes_accessed=pixels * chans * 20,
            transcendentals=0,
        ),
    )(received, slope, *([cube] * extra))


def backward_kernel(group, width, lag, *refs):
    now = refs[:group]
    left, right, clip, clip_before, spatial, grad, total, held = refs[group:]
    step = pl.program_id(1)
    rows, chans = grad.shape[2], grad.shape[3]
    for e in range(group):
        ext = step * group + e
        tiles = []
        for frame in range(2):
            tile = now[e][0, frame]
            tile = jnp.where(ext == 0, left[0, frame], tile)
            tiles.append(jnp.where(ext == width + 1, right[0, frame], tile))
        delta = lanes(tiles)
        above, below = row_shifts(delta.astype(jnp.float32), rows)
        for frame in range(2):
            at = slice(frame * chans, (frame + 1) * chans)
            held[step * group + e, frame] = lanes([below[:, at], delta[:, at], above[:, at]])

    @pl.when(step >= lag)
    def _():
        base = (step - lag) * group
        source = lanes([held[base + k].reshape(2 * rows, 3 * chans) for k in range(group + 2)])
        back = jnp.dot(source, spatial[...], preferred_element_type=jnp.float32)
        back = back.astype(jnp.bfloat16)
        for e in range(group):
            grad[e] = back[:, e * chans : (e + 1) * chans].reshape(2, rows, chans)
        ours = jnp.concatenate(
            [lanes([grad[e, frame] for frame in range(2)]) for e in range(group)], axis=0
        )
        taps = jnp.concatenate(
            [
                lanes([ref[e, frame] for ref in (clip_before, clip) for frame in range(2)])
                for e in range(group)
            ],
            axis=0,
        )
        term = lax.dot_general(
            ours, taps, (((0,), (0,)), ((), ())), preferred_element_type=jnp.float32
        )

        @pl.when(step == lag)
        def _():
            total[0] = term

        @pl.when(step > lag)
        def _():
            total[0] += term


def backward(delta, left, right, video, spatial, group):
    width, frames, rows, chans = video.shape
    lag = 2 // group
    steps = (width + 2) // group

    def own(e):
        return pl.BlockSpec(
            (1, 2, rows, chans),
            lambda p, j: (jnp.clip(j * group + e - 1, 0, width - 1), p, 0, 0),
        )

    edge = pl.BlockSpec((1, 2, rows, chans), lambda p, j: (0, p, 0, 0))
    pixels = width * frames * rows
    return pl.pallas_call(
        functools.partial(backward_kernel, group, width, lag),
        grid=(frames // 2, steps),
        in_specs=[own(e) for e in range(group)]
        + [
            edge,
            edge,
            pl.BlockSpec((group, 2, rows, chans), lambda p, j: (jnp.maximum(j - lag, 0), p, 0, 0)),
            pl.BlockSpec(
                (group, 2, rows, chans),
                lambda p, j: (jnp.maximum(j - lag, 0), jnp.maximum(p - 1, 0), 0, 0),
            ),
            pl.BlockSpec(spatial.shape, lambda p, j: (0, 0)),
        ],
        out_specs=[
            pl.BlockSpec(
                (group, 2, rows, chans), lambda p, j: (jnp.maximum(j - lag, 0), p, 0, 0)
            ),
            pl.BlockSpec((1, 2 * chans, 4 * chans), lambda p, j: (p, 0, 0)),
        ],
        out_shape=[
            jax.ShapeDtypeStruct((width, frames, rows, chans), jnp.bfloat16),
            jax.ShapeDtypeStruct((frames // 2, 2 * chans, 4 * chans), jnp.float32),
        ],
        scratch_shapes=[pltpu.VMEM((width + 2, 2, rows, 3 * chans), jnp.bfloat16)],
        compiler_params=pltpu.CompilerParams(vmem_limit_bytes=VMEM),
        cost_estimate=pl.CostEstimate(
            flops=pixels * chans * chans * 2 * 24,
            bytes_accessed=pixels * chans * 8,
            transcendentals=0,
        ),
    )(*([delta] * group), left, right, video, video, spatial)


def video_kernel(now, after, weights, out):
    cols, _, rows, chans = now.shape
    source = jnp.concatenate(
        [
            lanes([ref[e, frame] for ref in (now, after) for frame in range(2)])
            for e in range(cols)
        ],
        axis=0,
    )
    value = jnp.dot(source, weights[0], preferred_element_type=jnp.float32).astype(jnp.bfloat16)
    for e in range(cols):
        for frame in range(2):
            out[e, frame] = value[e * rows : (e + 1) * rows, frame * chans : (frame + 1) * chans]


def video_gradient(grad, weights):
    width, frames, rows, chans = grad.shape
    cols = 4 if width % 4 == 0 else 1
    last = frames // 2 - 1
    pixels = width * frames * rows
    return pl.pallas_call(
        video_kernel,
        grid=(frames // 2, width // cols),
        in_specs=[
            pl.BlockSpec((cols, 2, rows, chans), lambda p, i: (i, p, 0, 0)),
            pl.BlockSpec((cols, 2, rows, chans), lambda p, i: (i, jnp.minimum(p + 1, last), 0, 0)),
            pl.BlockSpec((1, 4 * chans, 2 * chans), lambda p, i: (p, 0, 0)),
        ],
        out_specs=pl.BlockSpec((cols, 2, rows, chans), lambda p, i: (i, p, 0, 0)),
        out_shape=jax.ShapeDtypeStruct(grad.shape, jnp.bfloat16),
        compiler_params=pltpu.CompilerParams(vmem_limit_bytes=VMEM),
        cost_estimate=pl.CostEstimate(
            flops=pixels * chans * chans * 2 * 6,
            bytes_accessed=pixels * chans * 6,
            transcendentals=0,
        ),
    )(grad, grad, weights)


def exchanged(axis, parts):
    count = lax.axis_size(axis)
    return [
        lax.ppermute(parts(s), axis, [(i, i ^ s) for i in range(count)]) for s in range(1, count)
    ]


def sum_over_devices(local):
    def scatter(value, axis):
        me = lax.axis_index(axis)
        blocks = value.reshape(lax.axis_size(axis), -1, value.shape[-1])
        pick = lambda s: lax.dynamic_index_in_dim(blocks, me ^ s, 0, keepdims=False)
        return functools.reduce(jnp.add, exchanged(axis, pick), pick(0))

    def spread(value, axis):
        count = lax.axis_size(axis)
        me = lax.axis_index(axis)
        parts = jnp.stack([value] + exchanged(axis, lambda s: value))
        order = jnp.arange(count, dtype=jnp.int32) ^ me
        return jnp.take(parts, order, axis=0).reshape(-1, value.shape[-1])

    value = scatter(scatter(local, "width"), "height")
    value = functools.reduce(jnp.add, exchanged("tm", lambda s: value), value)
    return spread(spread(value, "height"), "width")


def shards(video, out_grad, lengths, temporal_weight, spatial_weight):
    clip = video[0]
    width, frames, rows, chans = clip.shape
    n_tm = lax.axis_size("tm")
    n_height = lax.axis_size("height")
    frames_dev, rows_dev = out_grad.shape[2], out_grad.shape[3]
    assert frames_dev == 2
    total_cols = out_grad.shape[1] * lax.axis_size("width")
    group = 2 if width % 2 == 0 else 1
    pairs = frames // 2

    received = lax.all_to_all(out_grad[0], ("tm", "height"), split_axis=0, concat_axis=0, tiled=True)
    received = received.reshape(n_tm, n_height, width, frames_dev, rows_dev, chans)
    left, right = column_neighbours(clip[:1], clip[width - 1 :])

    masks = frame_masks(lengths, frames)
    paired = masks.reshape(3, pairs, 2)
    late = jnp.pad(paired, ((0, 0), (0, 1), (0, 0)))

    def tap_block(i, j):
        k = 2 + j - i
        return paired[k, :, j, None, None] * temporal_weight[k] if 0 <= k < 3 else None

    def back_block(i, j):
        k = i - j
        if not 0 <= k < 3:
            return None
        return late[k, i // 2 : i // 2 + pairs, i % 2, None, None] * temporal_weight[k].T

    temporal_mix = block_table(4, 2, tap_block)
    temporal_back = block_table(4, 2, back_block)

    def pre_block(i, j):
        b = i // 3 - j
        return spatial_weight[i % 3, b] if 0 <= b < 3 else None

    def grad_block(i, j):
        b = j + 2 - i // 3
        return spatial_weight[i % 3, b].T if 0 <= b < 3 else None

    spatial_mix = block_table(3 * (group + 2), group, pre_block)
    spatial_back = block_table(3 * (group + 2), group, grad_block)

    slope, cube = forward(clip, left, right, temporal_mix, spatial_mix, group)

    def edge_delta(col):
        grads = received[:, :, col].transpose(0, 2, 1, 3, 4).reshape(1, frames, rows, chans)
        return (grads.astype(jnp.float32) * slope[col][None]).astype(jnp.bfloat16)

    delta_left, delta_right = column_neighbours(edge_delta(0), edge_delta(width - 1))
    delta, spatial_terms = slopes(received, slope, cube, group)

    scale = float(frames * rows * total_cols) ** (-0.5)
    blocks = spatial_terms.reshape(group, chans, group + 2, 3, chans)
    spatial_local = jnp.stack(
        [sum(blocks[j, :, j + b] for j in range(group)) for b in range(3)], axis=2
    )
    spatial_local = (spatial_local * scale).transpose(1, 2, 3, 0).reshape(-1, chans)
    spatial_grad = sum_over_devices(spatial_local).reshape(3, 3, chans, chans)

    grad, temporal_terms = backward(delta, delta_left, delta_right, clip, spatial_back, group)
    video_grad = video_gradient(grad, temporal_back)

    blocks = temporal_terms.reshape(pairs, 2, chans, 4, chans)
    weights = paired.astype(jnp.float32) * scale
    temporal_local = jnp.stack(
        [
            sum(
                jnp.sum(weights[k, :, j, None, None] * blocks[:, j, :, 2 + j - k], axis=0)
                for j in range(2)
            ).T
            for k in range(3)
        ]
    )
    temporal_grad = sum_over_devices(temporal_local.reshape(-1, chans)).reshape(3, chans, chans)
    return video_grad[None], temporal_grad, spatial_grad


def solution(mesh):
    placed = (
        P("width", ("tm", "height"), None, None, None),
        P("width", None, "tm", "height", None),
        P(),
        P(),
        P(),
    )
    return jax.shard_map(
        shards,
        mesh=mesh,
        in_specs=placed,
        out_specs=(P("width", ("tm", "height"), None, None, None), P(), P()),
        check_vma=False,
    )
```

```python
import functools

import jax
import jax.numpy as jnp
from jax import lax
from jax.experimental import pallas as pl
from jax.experimental.pallas import tpu as pltpu
from jax.sharding import PartitionSpec as P

MESH_AXES = ("tm", "height", "width")
VMEM = 40 * 1024 * 1024


def frame_masks(lengths, frames):
    ends = jnp.cumsum(lengths, dtype=jnp.int32)
    starts = ends - lengths
    frame_index = jnp.arange(frames, dtype=jnp.int32)
    inside = (frame_index[:, None] >= starts[None, :]) & (frame_index[:, None] < ends[None, :])
    first = jnp.sum(jnp.where(inside, starts[None, :], 0), axis=1, dtype=jnp.int32)
    return jnp.stack([frame_index - lag >= first for lag in range(3)]).astype(jnp.bfloat16)


def column_neighbours(first, last):
    n_tm, n_height, n_width = (lax.axis_size(axis) for axis in MESH_AXES)
    blocks = n_tm * n_height
    place = [(pos % blocks) * n_width + pos // blocks for pos in range(blocks * n_width)]
    pairs = list(zip(place[:-1], place[1:]))
    left = lax.ppermute(last, MESH_AXES, pairs)
    right = lax.ppermute(first, MESH_AXES, [(b, a) for a, b in pairs])
    return left, right


def block_table(rows, cols, entry):
    blocks = [[entry(i, j) for j in range(cols)] for i in range(rows)]
    some = next(b for line in blocks for b in line if b is not None)
    zero = jnp.zeros_like(some)
    return jnp.concatenate(
        [jnp.concatenate([zero if b is None else b for b in line], axis=-1) for line in blocks],
        axis=-2,
    )


def row_shifts(block, rows):
    index = lax.broadcasted_iota(jnp.int32, block.shape, 0)
    above = jnp.where(index == 0, 0.0, pltpu.roll(block, 1, 0))
    below = jnp.where(index == rows - 1, 0.0, pltpu.roll(block, rows - 1, 0))
    return above.astype(jnp.bfloat16), below.astype(jnp.bfloat16)


def lanes(parts):
    return parts[0] if len(parts) == 1 else jnp.concatenate(parts, axis=1)


def forward_kernel(group, width, lag, *refs):
    now, before = refs[:group], refs[group : 2 * group]
    left, left_before, right, right_before, temporal, spatial, slope, act, held = refs[2 * group :]
    step = pl.program_id(1)
    rows, chans = slope.shape[2], slope.shape[3]
    sources = []
    for e in range(group):
        line = []
        for ours, l_ref, r_ref in ((before[e], left_before, right_before), (now[e], left, right)):
            for frame in range(2):
                tile = ours[0, frame]
                if e == 0:
                    tile = jnp.where(step == 0, l_ref[0, frame], tile)
                if e == group - 1:
                    tile = jnp.where(step * group + e == width + 1, r_ref[0, frame], tile)
                line.append(tile)
        sources.append(lanes(line))
    mixed = jnp.dot(
        jnp.concatenate(sources, axis=0), temporal[0], preferred_element_type=jnp.float32
    ).astype(jnp.bfloat16)
    for e in range(group):
        value = mixed[e * rows : (e + 1) * rows]
        above, below = row_shifts(value.astype(jnp.float32), rows)
        for frame in range(2):
            at = slice(frame * chans, (frame + 1) * chans)
            held[step * group + e, frame] = lanes([above[:, at], value[:, at], below[:, at]])

    @pl.when(step >= lag)
    def _():
        base = (step - lag) * group
        source = lanes([held[base + k].reshape(2 * rows, 3 * chans) for k in range(group + 2)])
        pre = jnp.dot(source, spatial[...], preferred_element_type=jnp.float32)
        sig = jax.nn.sigmoid(pre)
        value = sig * (1.0 + pre * (1.0 - sig))
        for e in range(group):
            slope[e] = value[:, e * chans : (e + 1) * chans].reshape(2, rows, chans)
            for frame in range(2):
                act[e, frame] = held[base + e + 1, frame, :, chans : 2 * chans]


def forward(video, left, right, temporal, spatial, group):
    width, frames, rows, chans = video.shape
    lag = 2 // group
    steps = (width + 2) // group

    def own(e, back):
        return pl.BlockSpec(
            (1, 2, rows, chans),
            lambda p, j: (
                jnp.clip(j * group + e - 1, 0, width - 1),
                jnp.maximum(p - back, 0),
                0,
                0,
            ),
        )

    def edge(back):
        return pl.BlockSpec((1, 2, rows, chans), lambda p, j: (0, jnp.maximum(p - back, 0), 0, 0))

    out = pl.BlockSpec((group, 2, rows, chans), lambda p, j: (jnp.maximum(j - lag, 0), p, 0, 0))
    pixels = width * frames * rows
    return pl.pallas_call(
        functools.partial(forward_kernel, group, width, lag),
        grid=(frames // 2, steps),
        in_specs=[own(e, 0) for e in range(group)]
        + [own(e, 1) for e in range(group)]
        + [
            edge(0),
            edge(1),
            edge(0),
            edge(1),
            pl.BlockSpec((1, 4 * chans, 2 * chans), lambda p, j: (p, 0, 0)),
            pl.BlockSpec(spatial.shape, lambda p, j: (0, 0)),
        ],
        out_specs=[out, out],
        out_shape=[
            jax.ShapeDtypeStruct((width, frames, rows, chans), jnp.float32),
            jax.ShapeDtypeStruct((width, frames, rows, chans), jnp.bfloat16),
        ],
        scratch_shapes=[pltpu.VMEM((width + 2, 2, rows, 3 * chans), jnp.bfloat16)],
        compiler_params=pltpu.CompilerParams(vmem_limit_bytes=VMEM),
        cost_estimate=pl.CostEstimate(
            flops=pixels * chans * chans * 2 * 24,
            bytes_accessed=pixels * chans * 14,
            transcendentals=pixels * chans,
        ),
    )(*([video] * (2 * group)), left, left, right, right, temporal, spatial)


def backward_kernel(group, inner, lag, scale, masks, *refs):
    edge_left, edge_right, left, right = refs[:4]
    refs = refs[4:]
    if inner:
        grads, slopes, refs = refs[0], refs[1 : 1 + group], refs[1 + group :]
    clip, clip_before, act, spatial, grad, sums, held, spatial_sum, temporal_sum = refs
    pair, step = pl.program_id(0), pl.program_id(1)
    last_pair, last = pl.num_programs(0) - 1, pl.num_programs(1) - 1
    rows, chans = grad.shape[2], grad.shape[3]

    def hold(e, delta):
        above, below = row_shifts(delta.astype(jnp.float32), rows)
        for frame in range(2):
            at = slice(frame * chans, (frame + 1) * chans)
            held[step * group + e, frame] = lanes([below[:, at], delta[:, at], above[:, at]])

    def hold_edges(tiles):
        for e, ref in enumerate(tiles):
            hold(e, lanes([ref[0, frame] for frame in range(2)]))

    @pl.when((pair == 0) & (step == 0))
    def _():
        spatial_sum[...] = jnp.zeros_like(spatial_sum)
        temporal_sum[...] = jnp.zeros_like(temporal_sum)

    @pl.when(step == 0)
    def _():
        hold_edges([left, edge_left][:group])

    @pl.when(step == last)
    def _():
        hold_edges([edge_right, right][-group:])

    @pl.when((step > 0) & (step < last))
    def _():
        if inner:
            bands, band = grads.shape[1], grads.shape[4]
            for e in range(group):
                hold(
                    e,
                    jnp.concatenate(
                        [
                            lanes(
                                [
                                    (
                                        grads[0, b, e, frame].astype(jnp.float32)
                                        * slopes[e][0, frame, b * band : (b + 1) * band]
                                    ).astype(jnp.bfloat16)
                                    for frame in range(2)
                                ]
                            )
                            for b in range(bands)
                        ],
                        axis=0,
                    ),
                )
        else:
            hold_edges([edge_left])

    @pl.when(step >= lag)
    def _():
        base = (step - lag) * group
        source = lanes([held[base + k].reshape(2 * rows, 3 * chans) for k in range(group + 2)])
        back = jnp.dot(source, spatial[...], preferred_element_type=jnp.float32)
        back = back.astype(jnp.bfloat16)
        for e in range(group):
            grad[e] = back[:, e * chans : (e + 1) * chans].reshape(2, rows, chans)
        own = lanes([act[e].reshape(2 * rows, chans) for e in range(group)])
        spatial_sum[...] += lax.dot_general(
            own, source, (((0,), (0,)), ((), ())), preferred_element_type=jnp.float32
        )
        ours = jnp.concatenate(
            [
                lanes(
                    [
                        back[f * rows : (f + 1) * rows, e * chans : (e + 1) * chans]
                        for f in range(2)
                    ]
                )
                for e in range(group)
            ],
            axis=0,
        )
        taps = jnp.concatenate(
            [
                lanes([ref[e, frame] for ref in (clip_before, clip) for frame in range(2)])
                for e in range(group)
            ],
            axis=0,
        )
        term = lax.dot_general(
            ours, taps, (((0,), (0,)), ((), ())), preferred_element_type=jnp.float32
        )
        for k in range(3):
            temporal_sum[k] += sum(
                masks[k, 2 * pair + j]
                * term[j * chans : (j + 1) * chans, (2 + j - k) * chans : (3 + j - k) * chans]
                for j in range(2)
            )

    @pl.when((pair == last_pair) & (step == last))
    def _():
        for k in range(3):
            sums[k] = temporal_sum[k].T * scale
        for a in range(3):
            for b in range(3):
                value = sum(
                    spatial_sum[
                        j * chans : (j + 1) * chans,
                        ((j + 2 - b) * 3 + a) * chans : ((j + 2 - b) * 3 + a + 1) * chans,
                    ]
                    for j in range(group)
                )
                sums[3 + 3 * a + b] = value * scale


def backward(edges, left, right, inner, slope, video, act, masks, spatial, scale, group):
    width, frames, rows, chans = video.shape
    lag = 2 // group
    steps = (width + 2) // group

    def single(place):
        return pl.BlockSpec((1, 2, rows, chans), lambda p, j, m: (place(j), p, 0, 0))

    def pair(back):
        return pl.BlockSpec(
            (group, 2, rows, chans),
            lambda p, j, m: (jnp.maximum(j - lag, 0), jnp.maximum(p - back, 0), 0, 0),
        )

    if group == 1:
        in_specs = [single(lambda j: jnp.clip(j - 1, 0, width - 1)), single(lambda j: width - 1)]
    else:
        in_specs = [single(lambda j: 0), single(lambda j: 1)]
    in_specs += [single(lambda j: 0), single(lambda j: 0)]
    operands = [edges, edges, left, right]
    if inner is not None:
        bands, band = inner.shape[1], inner.shape[4]
        blocks = inner.shape[2] // group
        in_specs.append(
            pl.BlockSpec(
                (1, bands, group, 2, band, chans),
                lambda p, j, m: (p, 0, jnp.clip(j - 1, 0, blocks - 1), 0, 0, 0),
            )
        )
        in_specs += [
            single(functools.partial(lambda e, j: jnp.clip(j * group + e - 1, 0, width - 1), e))
            for e in range(group)
        ]
        operands += [inner] + [slope] * group
    in_specs += [
        pair(0),
        pair(1),
        pair(0),
        pl.BlockSpec(spatial.shape, lambda p, j, m: (0, 0)),
    ]
    operands += [video, video, act, spatial]
    pixels = width * frames * rows
    return pl.pallas_call(
        functools.partial(backward_kernel, group, inner is not None, lag, scale),
        grid_spec=pltpu.PrefetchScalarGridSpec(
            num_scalar_prefetch=1,
            grid=(frames // 2, steps),
            in_specs=in_specs,
            out_specs=[
                pair(0),
                pl.BlockSpec((12, chans, chans), lambda p, j, m: (0, 0, 0)),
            ],
            scratch_shapes=[
                pltpu.VMEM((width + 2, 2, rows, 3 * chans), jnp.bfloat16),
                pltpu.VMEM((group * chans, (group + 2) * 3 * chans), jnp.float32),
                pltpu.VMEM((3, chans, chans), jnp.float32),
            ],
        ),
        out_shape=[
            jax.ShapeDtypeStruct((width, frames, rows, chans), jnp.bfloat16),
            jax.ShapeDtypeStruct((12, chans, chans), jnp.float32),
        ],
        compiler_params=pltpu.CompilerParams(vmem_limit_bytes=VMEM),
        cost_estimate=pl.CostEstimate(
            flops=pixels * chans * chans * 2 * 40,
            bytes_accessed=pixels * chans * 14,
            transcendentals=0,
        ),
    )(masks, *operands)


def video_kernel(now, after, weights, out):
    cols, _, rows, chans = now.shape
    source = jnp.concatenate(
        [
            lanes([ref[e, frame] for ref in (now, after) for frame in range(2)])
            for e in range(cols)
        ],
        axis=0,
    )
    value = jnp.dot(source, weights[0], preferred_element_type=jnp.float32).astype(jnp.bfloat16)
    for e in range(cols):
        for frame in range(2):
            out[e, frame] = value[e * rows : (e + 1) * rows, frame * chans : (frame + 1) * chans]


def video_gradient(grad, weights):
    width, frames, rows, chans = grad.shape
    cols = 4 if width % 4 == 0 else 1
    last = frames // 2 - 1
    pixels = width * frames * rows
    return pl.pallas_call(
        video_kernel,
        grid=(frames // 2, width // cols),
        in_specs=[
            pl.BlockSpec((cols, 2, rows, chans), lambda p, i: (i, p, 0, 0)),
            pl.BlockSpec((cols, 2, rows, chans), lambda p, i: (i, jnp.minimum(p + 1, last), 0, 0)),
            pl.BlockSpec((1, 4 * chans, 2 * chans), lambda p, i: (p, 0, 0)),
        ],
        out_specs=pl.BlockSpec((cols, 2, rows, chans), lambda p, i: (i, p, 0, 0)),
        out_shape=jax.ShapeDtypeStruct(grad.shape, jnp.bfloat16),
        compiler_params=pltpu.CompilerParams(vmem_limit_bytes=VMEM),
        cost_estimate=pl.CostEstimate(
            flops=pixels * chans * chans * 2 * 6,
            bytes_accessed=pixels * chans * 6,
            transcendentals=0,
        ),
    )(grad, grad, weights)


def exchanged(axis, parts):
    count = lax.axis_size(axis)
    return [
        lax.ppermute(parts(s), axis, [(i, i ^ s) for i in range(count)]) for s in range(1, count)
    ]


def sum_over_devices(local):
    def scatter(value, axis):
        me = lax.axis_index(axis)
        blocks = value.reshape(lax.axis_size(axis), -1, value.shape[-1])
        pick = lambda s: lax.dynamic_index_in_dim(blocks, me ^ s, 0, keepdims=False)
        return functools.reduce(jnp.add, exchanged(axis, pick), pick(0))

    def spread(value, axis):
        count = lax.axis_size(axis)
        me = lax.axis_index(axis)
        parts = jnp.stack([value] + exchanged(axis, lambda s: value))
        order = jnp.arange(count, dtype=jnp.int32) ^ me
        return jnp.take(parts, order, axis=0).reshape(-1, value.shape[-1])

    value = scatter(scatter(local, "width"), "height")
    value = functools.reduce(jnp.add, exchanged("tm", lambda s: value), value)
    return spread(spread(value, "height"), "width")


def shards(video, out_grad, lengths, temporal_weight, spatial_weight):
    clip = video[0]
    width, frames, rows, chans = clip.shape
    n_tm = lax.axis_size("tm")
    n_height = lax.axis_size("height")
    frames_dev, rows_dev = out_grad.shape[2], out_grad.shape[3]
    assert frames_dev == 2
    total_cols = out_grad.shape[1] * lax.axis_size("width")
    group = 2 if width % 2 == 0 else 1
    pairs = frames // 2

    left, right = column_neighbours(clip[:1], clip[width - 1 :])
    blocks = out_grad[0].reshape(n_tm * n_height, width, frames_dev, rows_dev, chans)

    def to_columns(part):
        got = lax.all_to_all(part, ("tm", "height"), split_axis=0, concat_axis=0, tiled=True)
        return got.reshape(n_tm, n_height, *part.shape[1:])

    inner = None
    if group == 2 and width > 2:
        outer = to_columns(jnp.stack([blocks[:, 0], blocks[:, width - 1]], axis=1))
        inner = blocks[:, 1 : width - 1]
        inner, outer = lax.optimization_barrier((inner, outer))
        inner = to_columns(inner)
    else:
        outer = to_columns(blocks)

    masks = frame_masks(lengths, frames)
    paired = masks.reshape(3, pairs, 2)
    late = jnp.pad(paired, ((0, 0), (0, 1), (0, 0)))

    def tap_block(i, j):
        k = 2 + j - i
        return paired[k, :, j, None, None] * temporal_weight[k] if 0 <= k < 3 else None

    def back_block(i, j):
        k = i - j
        if not 0 <= k < 3:
            return None
        return late[k, i // 2 : i // 2 + pairs, i % 2, None, None] * temporal_weight[k].T

    temporal_mix = block_table(4, 2, tap_block)
    temporal_back = block_table(4, 2, back_block)

    def pre_block(i, j):
        b = i // 3 - j
        return spatial_weight[i % 3, b] if 0 <= b < 3 else None

    def grad_block(i, j):
        b = j + 2 - i // 3
        return spatial_weight[i % 3, b].T if 0 <= b < 3 else None

    spatial_mix = block_table(3 * (group + 2), group, pre_block)
    spatial_back = block_table(3 * (group + 2), group, grad_block)

    slope, act = forward(clip, left, right, temporal_mix, spatial_mix, group)

    count = outer.shape[2]
    grads = outer.transpose(2, 0, 3, 1, 4, 5).reshape(count, frames, rows, chans)
    slopes = slope if count == width else jnp.stack([slope[0], slope[width - 1]])
    edges = (grads.astype(jnp.float32) * slopes).astype(jnp.bfloat16)
    delta_left, delta_right = column_neighbours(edges[:1], edges[count - 1 :])

    scale = float(frames * rows * total_cols) ** (-0.5)
    grad, local = backward(
        edges,
        delta_left,
        delta_right,
        inner,
        slope,
        clip,
        act,
        masks.astype(jnp.float32),
        spatial_back,
        scale,
        group,
    )
    video_grad = video_gradient(grad, temporal_back)
    sums = sum_over_devices(local.reshape(-1, chans)).reshape(12, chans, chans)
    temporal_grad, spatial_grad = sums[:3], sums[3:].reshape(3, 3, chans, chans)
    return video_grad[None], temporal_grad, spatial_grad


def solution(mesh):
    placed = (
        P("width", ("tm", "height"), None, None, None),
        P("width", None, "tm", "height", None),
        P(),
        P(),
        P(),
    )
    return jax.shard_map(
        shards,
        mesh=mesh,
        in_specs=placed,
        out_specs=(P("width", ("tm", "height"), None, None, None), P(), P()),
        check_vma=False,
    )
```

```python
import functools

import jax
import jax.numpy as jnp
from jax import lax
from jax.experimental import pallas as pl
from jax.experimental.pallas import tpu as pltpu
from jax.sharding import PartitionSpec as P

MESH_AXES = ("tm", "height", "width")
VMEM = 40 * 1024 * 1024


def frame_masks(lengths, frames):
    ends = jnp.cumsum(lengths, dtype=jnp.int32)
    starts = ends - lengths
    frame_index = jnp.arange(frames, dtype=jnp.int32)
    inside = (frame_index[:, None] >= starts[None, :]) & (frame_index[:, None] < ends[None, :])
    first = jnp.sum(jnp.where(inside, starts[None, :], 0), axis=1, dtype=jnp.int32)
    return jnp.stack([frame_index - lag >= first for lag in range(3)]).astype(jnp.bfloat16)


def column_neighbours(first, last):
    n_tm, n_height, n_width = (lax.axis_size(axis) for axis in MESH_AXES)
    blocks = n_tm * n_height
    place = [(pos % blocks) * n_width + pos // blocks for pos in range(blocks * n_width)]
    pairs = list(zip(place[:-1], place[1:]))
    left = lax.ppermute(last, MESH_AXES, pairs)
    right = lax.ppermute(first, MESH_AXES, [(b, a) for a, b in pairs])
    return left, right


def block_table(rows, cols, entry):
    blocks = [[entry(i, j) for j in range(cols)] for i in range(rows)]
    some = next(b for line in blocks for b in line if b is not None)
    zero = jnp.zeros_like(some)
    return jnp.concatenate(
        [jnp.concatenate([zero if b is None else b for b in line], axis=-1) for line in blocks],
        axis=-2,
    )


def row_shifts(block, rows):
    index = lax.broadcasted_iota(jnp.int32, block.shape, 0)
    above = jnp.where(index == 0, 0.0, pltpu.roll(block, 1, 0))
    below = jnp.where(index == rows - 1, 0.0, pltpu.roll(block, rows - 1, 0))
    return above.astype(jnp.bfloat16), below.astype(jnp.bfloat16)


def lanes(parts):
    return parts[0] if len(parts) == 1 else jnp.concatenate(parts, axis=1)


def forward_kernel(group, width, lag, *refs):
    now, before = refs[:group], refs[group : 2 * group]
    left, left_before, right, right_before, temporal, spatial, slope, turned, held = refs[2 * group :]
    step = pl.program_id(1)
    rows, chans = slope.shape[2], slope.shape[3]
    sources = []
    for e in range(group):
        line = []
        for ours, l_ref, r_ref in ((before[e], left_before, right_before), (now[e], left, right)):
            for frame in range(2):
                tile = ours[0, frame]
                if e == 0:
                    tile = jnp.where(step == 0, l_ref[0, frame], tile)
                if e == group - 1:
                    tile = jnp.where(step * group + e == width + 1, r_ref[0, frame], tile)
                line.append(tile)
                if ours is now[e]:
                    turned[e, frame] = tile.T
        sources.append(lanes(line))
    mixed = jnp.dot(
        jnp.concatenate(sources, axis=0), temporal[0], preferred_element_type=jnp.float32
    ).astype(jnp.bfloat16)
    for e in range(group):
        value = mixed[e * rows : (e + 1) * rows]
        above, below = row_shifts(value.astype(jnp.float32), rows)
        for frame in range(2):
            at = slice(frame * chans, (frame + 1) * chans)
            held[step * group + e, frame] = lanes([above[:, at], value[:, at], below[:, at]])

    @pl.when(step >= lag)
    def _():
        base = (step - lag) * group
        source = lanes([held[base + k].reshape(2 * rows, 3 * chans) for k in range(group + 2)])
        pre = jnp.dot(source, spatial[...], preferred_element_type=jnp.float32)
        sig = jax.nn.sigmoid(pre)
        value = sig * (1.0 + pre * (1.0 - sig))
        for e in range(group):
            slope[e] = value[:, e * chans : (e + 1) * chans].reshape(2, rows, chans)


def forward(video, left, right, temporal, spatial, group):
    width, frames, rows, chans = video.shape
    lag = 2 // group
    steps = (width + 2) // group

    def own(e, back):
        return pl.BlockSpec(
            (1, 2, rows, chans),
            lambda p, j: (
                jnp.clip(j * group + e - 1, 0, width - 1),
                jnp.maximum(p - back, 0),
                0,
                0,
            ),
        )

    def edge(back):
        return pl.BlockSpec((1, 2, rows, chans), lambda p, j: (0, jnp.maximum(p - back, 0), 0, 0))

    out = pl.BlockSpec((group, 2, rows, chans), lambda p, j: (jnp.maximum(j - lag, 0), p, 0, 0))
    pixels = width * frames * rows
    return pl.pallas_call(
        functools.partial(forward_kernel, group, width, lag),
        grid=(frames // 2, steps),
        in_specs=[own(e, 0) for e in range(group)]
        + [own(e, 1) for e in range(group)]
        + [
            edge(0),
            edge(1),
            edge(0),
            edge(1),
            pl.BlockSpec((1, 4 * chans, 2 * chans), lambda p, j: (p, 0, 0)),
            pl.BlockSpec(spatial.shape, lambda p, j: (0, 0)),
        ],
        out_specs=[out, pl.BlockSpec((group, 2, chans, rows), lambda p, j: (j, p, 0, 0))],
        out_shape=[
            jax.ShapeDtypeStruct((width, frames, rows, chans), jnp.float32),
            jax.ShapeDtypeStruct((width + 2, frames, chans, rows), jnp.bfloat16),
        ],
        scratch_shapes=[pltpu.VMEM((width + 2, 2, rows, 3 * chans), jnp.bfloat16)],
        compiler_params=pltpu.CompilerParams(vmem_limit_bytes=VMEM),
        cost_estimate=pl.CostEstimate(
            flops=pixels * chans * chans * 2 * 24,
            bytes_accessed=pixels * chans * 14,
            transcendentals=pixels * chans,
        ),
    )(*([video] * (2 * group)), left, left, right, right, temporal, spatial)


def moments_kernel(group, span, extra, scale, masks, *refs):
    grads, slope = refs[:2]
    now, before = refs[2 : 2 + extra], refs[2 + extra : 2 + 2 * extra]
    temporal, spatial, delta, sums, total = refs[2 + 2 * extra :]
    pair, step = pl.program_id(0), pl.program_id(1)
    bands, band = grads.shape[1], grads.shape[4]
    rows, chans = slope.shape[2], slope.shape[3]

    @pl.when((pair == 0) & (step == 0))
    def _():
        total[...] = jnp.zeros_like(total)

    places = [(n, frame) for n in range(span) for frame in range(2)]
    triples = []
    for n, frame in places:
        line = []
        for e in range(n * group, (n + 1) * group):
            for b in range(bands):
                at = slice(b * band, (b + 1) * band)
                value = grads[0, b, e, frame].astype(jnp.float32) * slope[e, frame, at]
                delta[e, frame, at] = value.astype(jnp.bfloat16)
            value = delta[e, frame]
            above, below = row_shifts(value.astype(jnp.float32), rows)
            line += [below, value, above]
        triples.append(lanes(line))
    right = jnp.concatenate(triples, axis=0)

    def add(lag, left):
        total[lag] += jnp.dot(left, right, preferred_element_type=jnp.float32)

    def turned(refs, n, frame):
        cols = range(n * group, (n + 1) * group + 2)
        return jnp.concatenate([refs[c // group][c % group, frame] for c in cols], axis=0)

    add(0, lanes([turned(now, n, frame) for n, frame in places]))
    for lag in (1, 2):
        keep = [masks[lag, 2 * pair + frame] for frame in range(2)]
        source = [(before, 1), (now, 0)] if lag == 1 else [(before, 0), (before, 1)]

        @pl.when(keep[0] + keep[1] > 0)
        def _():
            left = []
            for n, frame in places:
                refs, other = source[frame]
                value = turned(refs, n, other)
                left.append(jnp.where(keep[frame] > 0, value, jnp.zeros_like(value)))
            add(lag, lanes(left))

    @pl.when((pair == pl.num_programs(0) - 1) & (step == pl.num_programs(1) - 1))
    def _():
        lines = []
        for lag in range(3):
            line = []
            for a in range(3):
                for b in range(3):
                    line.append(
                        sum(
                            total[
                                lag,
                                (j + b) * chans : (j + b + 1) * chans,
                                (j * 3 + a) * chans : (j * 3 + a + 1) * chans,
                            ]
                            for j in range(group)
                        )
                    )
            lines.append(lanes(line))
        moments = jnp.concatenate(lines, axis=0)
        high = moments.astype(jnp.bfloat16)
        low = (moments - high.astype(jnp.float32)).astype(jnp.bfloat16)

        def product(left, right):
            return jnp.dot(left, right, preferred_element_type=jnp.float32)

        spatial_sum = product(temporal[...], high) + product(temporal[...], low)
        temporal_sum = product(high, spatial[...]) + product(low, spatial[...])
        for k in range(3):
            sums[k] = temporal_sum[k * chans : (k + 1) * chans] * scale
        for k in range(9):
            sums[3 + k] = spatial_sum[:, k * chans : (k + 1) * chans] * scale


def moments(received, slope, turned, masks, temporal, spatial, scale, group):
    width, frames, rows, chans = slope.shape
    bands, band = received.shape[1], received.shape[4]
    span = 2 if width % (2 * group) == 0 else 1
    cols = span * group
    extra = span + 2 // group
    pixels = width * frames * rows

    def columns(k, back):
        return pl.BlockSpec(
            (group, 2, chans, rows),
            lambda p, i, m: (i * span + k, jnp.maximum(p - back, 0), 0, 0),
        )

    own = pl.BlockSpec((cols, 2, rows, chans), lambda p, i, m: (i, p, 0, 0))
    return pl.pallas_call(
        functools.partial(moments_kernel, group, span, extra, scale),
        grid_spec=pltpu.PrefetchScalarGridSpec(
            num_scalar_prefetch=1,
            grid=(frames // 2, width // cols),
            in_specs=[
                pl.BlockSpec((1, bands, cols, 2, band, chans), lambda p, i, m: (p, 0, i, 0, 0, 0)),
                own,
            ]
            + [columns(k, 0) for k in range(extra)]
            + [columns(k, 1) for k in range(extra)]
            + [
                pl.BlockSpec(temporal.shape, lambda p, i, m: (0, 0)),
                pl.BlockSpec(spatial.shape, lambda p, i, m: (0, 0)),
            ],
            out_specs=[own, pl.BlockSpec((12, chans, chans), lambda p, i, m: (0, 0, 0))],
            scratch_shapes=[
                pltpu.VMEM((3, (group + 2) * chans, group * 3 * chans), jnp.float32),
            ],
        ),
        out_shape=[
            jax.ShapeDtypeStruct((width, frames, rows, chans), jnp.bfloat16),
            jax.ShapeDtypeStruct((12, chans, chans), jnp.float32),
        ],
        compiler_params=pltpu.CompilerParams(vmem_limit_bytes=VMEM),
        cost_estimate=pl.CostEstimate(
            flops=pixels * chans * chans * 2 * 30,
            bytes_accessed=pixels * chans * 20,
            transcendentals=0,
        ),
    )(masks, received, slope, *([turned] * (2 * extra)), temporal, spatial)


def backward_kernel(group, *refs):
    delta, left, right, spatial = refs[:4]
    grad = refs[-1]
    width, rows, chans = grad.shape[0], grad.shape[2], grad.shape[3]
    triples = []
    for col in [left.at[0]] + [delta.at[c] for c in range(width)] + [right.at[0]]:
        lines = []
        for frame in range(2):
            value = col[frame]
            above, below = row_shifts(value.astype(jnp.float32), rows)
            lines.append(lanes([below, value, above]))
        triples.append(jnp.concatenate(lines, axis=0))
    for base in range(0, width, group):
        source = lanes(triples[base : base + group + 2])
        back = jnp.dot(source, spatial[...], preferred_element_type=jnp.float32)
        back = back.astype(jnp.bfloat16)
        for e in range(group):
            grad[base + e] = back[:, e * chans : (e + 1) * chans].reshape(2, rows, chans)


def backward(delta, left, right, spatial, filled, pairs, group):
    width, _, rows, chans = delta.shape
    start = pairs[0]
    filled = [] if filled is None else [filled]
    block = pl.BlockSpec((width, 2, rows, chans), lambda p: (0, start + p, 0, 0))
    edge = pl.BlockSpec((1, 2, rows, chans), lambda p: (0, start + p, 0, 0))
    pixels = width * 2 * len(pairs) * rows
    return pl.pallas_call(
        functools.partial(backward_kernel, group),
        grid=(len(pairs),),
        in_specs=[block, edge, edge, pl.BlockSpec(spatial.shape, lambda p: (0, 0))]
        + [pl.BlockSpec(memory_space=pl.ANY)] * len(filled),
        out_specs=block,
        out_shape=jax.ShapeDtypeStruct(delta.shape, jnp.bfloat16),
        input_output_aliases={4: 0} if filled else {},
        compiler_params=pltpu.CompilerParams(vmem_limit_bytes=VMEM),
        cost_estimate=pl.CostEstimate(
            flops=pixels * chans * chans * 2 * 18,
            bytes_accessed=pixels * chans * 6,
            transcendentals=0,
        ),
    )(delta, left, right, spatial, *filled)


def video_kernel(now, after, weights, out):
    cols, _, rows, chans = now.shape
    source = jnp.concatenate(
        [
            lanes([ref[e, frame] for ref in (now, after) for frame in range(2)])
            for e in range(cols)
        ],
        axis=0,
    )
    value = jnp.dot(source, weights[0], preferred_element_type=jnp.float32).astype(jnp.bfloat16)
    for e in range(cols):
        for frame in range(2):
            out[e, frame] = value[e * rows : (e + 1) * rows, frame * chans : (frame + 1) * chans]


def video_gradient(grad, weights):
    width, frames, rows, chans = grad.shape
    cols = 4 if width % 4 == 0 else 1
    last = frames // 2 - 1
    pixels = width * frames * rows
    return pl.pallas_call(
        video_kernel,
        grid=(frames // 2, width // cols),
        in_specs=[
            pl.BlockSpec((cols, 2, rows, chans), lambda p, i: (i, p, 0, 0)),
            pl.BlockSpec((cols, 2, rows, chans), lambda p, i: (i, jnp.minimum(p + 1, last), 0, 0)),
            pl.BlockSpec((1, 4 * chans, 2 * chans), lambda p, i: (p, 0, 0)),
        ],
        out_specs=pl.BlockSpec((cols, 2, rows, chans), lambda p, i: (i, p, 0, 0)),
        out_shape=jax.ShapeDtypeStruct(grad.shape, jnp.bfloat16),
        compiler_params=pltpu.CompilerParams(vmem_limit_bytes=VMEM),
        cost_estimate=pl.CostEstimate(
            flops=pixels * chans * chans * 2 * 6,
            bytes_accessed=pixels * chans * 6,
            transcendentals=0,
        ),
    )(grad, grad, weights)


def exchanged(axis, parts):
    count = lax.axis_size(axis)
    return [
        lax.ppermute(parts(s), axis, [(i, i ^ s) for i in range(count)]) for s in range(1, count)
    ]


def sum_over_devices(local, works, state):
    def pieces(value, axis):
        me = lax.axis_index(axis)
        blocks = value.reshape(lax.axis_size(axis), -1, value.shape[-1])
        return lambda s: lax.dynamic_index_in_dim(blocks, me ^ s, 0, keepdims=False)

    def spread(parts, axis):
        order = jnp.arange(len(parts), dtype=jnp.int32) ^ lax.axis_index(axis)
        return jnp.take(jnp.stack(parts), order, axis=0).reshape(-1, parts[0].shape[-1])

    def beside(value, got, work, state):
        value, state = lax.optimization_barrier((value, state))
        got = got(value)
        state = work(state)
        got, state = lax.optimization_barrier((got, state))
        return value, got, state

    pick = pieces(local, "width")
    value = functools.reduce(jnp.add, exchanged("width", pick), pick(0))
    value, got, state = beside(
        value, lambda v: exchanged("height", pieces(v, "height")), works[0], state
    )
    value = functools.reduce(jnp.add, got, pieces(value, "height")(0))
    value, got, state = beside(
        value, lambda v: exchanged("tm", lambda s: v), works[1], state
    )
    value = functools.reduce(jnp.add, got, value)
    value, got, state = beside(
        value, lambda v: exchanged("height", lambda s: v), works[2], state
    )
    value = spread([value] + got, "height")
    return spread([value] + exchanged("width", lambda s: value), "width"), state


def shards(video, out_grad, lengths, temporal_weight, spatial_weight):
    clip = video[0]
    width, frames, rows, chans = clip.shape
    n_tm = lax.axis_size("tm")
    n_height = lax.axis_size("height")
    frames_dev, rows_dev = out_grad.shape[2], out_grad.shape[3]
    assert frames_dev == 2
    total_cols = out_grad.shape[1] * lax.axis_size("width")
    group = 2 if width % 2 == 0 else 1
    pairs = frames // 2

    left, right = column_neighbours(clip[:1], clip[width - 1 :])
    received = lax.all_to_all(out_grad[0], ("tm", "height"), split_axis=0, concat_axis=0, tiled=True)
    received = received.reshape(n_tm, n_height, width, frames_dev, rows_dev, chans)

    masks = frame_masks(lengths, frames)
    paired = masks.reshape(3, pairs, 2)
    late = jnp.pad(paired, ((0, 0), (0, 1), (0, 0)))

    def tap_block(i, j):
        k = 2 + j - i
        return paired[k, :, j, None, None] * temporal_weight[k] if 0 <= k < 3 else None

    def back_block(i, j):
        k = i - j
        if not 0 <= k < 3:
            return None
        return late[k, i // 2 : i // 2 + pairs, i % 2, None, None] * temporal_weight[k].T

    temporal_mix = block_table(4, 2, tap_block)
    temporal_back = block_table(4, 2, back_block)

    def pre_block(i, j):
        b = i // 3 - j
        return spatial_weight[i % 3, b] if 0 <= b < 3 else None

    def grad_block(i, j):
        b = j + 2 - i // 3
        return spatial_weight[i % 3, b].T if 0 <= b < 3 else None

    spatial_mix = block_table(3 * (group + 2), group, pre_block)
    spatial_back = block_table(3 * (group + 2), group, grad_block)

    slope, turned = forward(clip, left, right, temporal_mix, spatial_mix, group)

    def edge_delta(col):
        grads = received[:, :, col].transpose(0, 2, 1, 3, 4).reshape(1, frames, rows, chans)
        return (grads.astype(jnp.float32) * slope[col][None]).astype(jnp.bfloat16)

    first, last = edge_delta(0), edge_delta(width - 1)
    received, first, last = lax.optimization_barrier((received, first, last))
    delta_left, delta_right = column_neighbours(first, last)

    scale = float(frames * rows * total_cols) ** (-0.5)
    delta, local = moments(
        received,
        slope,
        turned,
        masks.astype(jnp.float32),
        jnp.concatenate([temporal_weight[k].T for k in range(3)], axis=1),
        jnp.concatenate([spatial_weight[k // 3, k % 3].T for k in range(9)], axis=0),
        scale,
        group,
    )
    local, delta, delta_left, delta_right = lax.optimization_barrier(
        (local, delta, delta_left, delta_right)
    )

    half = pairs // 2

    def first_half(state):
        grad = backward(*state, spatial_back, None, range(half), group)
        return grad, state

    def second_half(both):
        grad, state = both
        return backward(*state, spatial_back, grad, range(half, pairs), group)

    sums, video_grad = sum_over_devices(
        local.reshape(-1, chans),
        [first_half, second_half, lambda grad: video_gradient(grad, temporal_back)],
        (delta, delta_left, delta_right),
    )
    sums = sums.reshape(12, chans, chans)
    temporal_grad, spatial_grad = sums[:3], sums[3:].reshape(3, 3, chans, chans)
    return video_grad[None], temporal_grad, spatial_grad


def solution(mesh):
    placed = (
        P("width", ("tm", "height"), None, None, None),
        P("width", None, "tm", "height", None),
        P(),
        P(),
        P(),
    )
    return jax.shard_map(
        shards,
        mesh=mesh,
        in_specs=placed,
        out_specs=(P("width", ("tm", "height"), None, None, None), P(), P()),
        check_vma=False,
    )
```

```python
import functools

import jax
import jax.numpy as jnp
from jax import lax
from jax.experimental import pallas as pl
from jax.experimental.pallas import tpu as pltpu
from jax.sharding import PartitionSpec as P

MESH_AXES = ("tm", "height", "width")
MIB = 1024 * 1024


def column_neighbours(first, last):
    n_tm, n_height, n_width = (lax.axis_size(axis) for axis in MESH_AXES)
    blocks = n_tm * n_height
    place = [(pos % blocks) * n_width + pos // blocks for pos in range(blocks * n_width)]
    pairs = list(zip(place[:-1], place[1:]))
    left = lax.ppermute(last, MESH_AXES, pairs)
    right = lax.ppermute(first, MESH_AXES, [(b, a) for a, b in pairs])
    return left, right


def prepare_kernel(group, lengths, temporal, spatial, *outs):
    mix, back, pre, grad, temporal_turned, spatial_turned, masks = outs
    frames, chans = masks.shape[1], temporal.shape[1]
    end, spans = jnp.int32(0), []
    for n in range(lengths.shape[0]):
        spans.append((end, end + lengths[n]))
        end = end + lengths[n]
    keep = []
    for frame in range(frames):
        first = jnp.int32(0)
        for start, stop in spans:
            first = first + jnp.where((frame >= start) & (frame < stop), start, 0)
        keep.append([jnp.where(frame - lag >= first, 1.0, 0.0) for lag in range(3)])
    for lag in range(3):
        for frame in range(frames):
            masks[lag, frame] = keep[frame][lag]

    zero = jnp.zeros((chans, chans), jnp.bfloat16)
    turned = [temporal[k].T for k in range(3)]
    for i in range(4):
        for j in range(2):
            at = (slice(i * chans, (i + 1) * chans), slice(j * chans, (j + 1) * chans))
            for p in range(frames // 2):
                k, frame = 2 + j - i, 2 * p + j
                value = zero
                if 0 <= k < 3:
                    value = jnp.where(keep[frame][k] > 0, temporal[k], zero)
                mix[(p, *at)] = value
                k, frame = i - j, 2 * p + i
                value = zero
                if 0 <= k < 3 and frame < frames:
                    value = jnp.where(keep[frame][k] > 0, turned[k], zero)
                back[(p, *at)] = value
    for k in range(3):
        temporal_turned[:, k * chans : (k + 1) * chans] = turned[k]
    for a in range(3):
        for b in range(3):
            value = spatial[a, b].T
            n = 3 * a + b
            spatial_turned[n * chans : (n + 1) * chans] = value
            for j in range(group):
                at = slice(j * chans, (j + 1) * chans)
                i = 3 * (b + j) + a
                pre[i * chans : (i + 1) * chans, at] = spatial[a, b]
                i = 3 * (j + 2 - b) + a
                grad[i * chans : (i + 1) * chans, at] = value
    for j in range(group):
        for i in range(group + 2):
            if not 0 <= i - j < 3:
                at = (slice(3 * i * chans, 3 * (i + 1) * chans), slice(j * chans, (j + 1) * chans))
                pre[at] = jnp.zeros((3 * chans, chans), jnp.bfloat16)
                grad[at] = jnp.zeros((3 * chans, chans), jnp.bfloat16)


def prepare(lengths, temporal, spatial, frames, group):
    chans = temporal.shape[1]

    def wide(*shape):
        return jax.ShapeDtypeStruct(shape, jnp.bfloat16)

    vmem, smem = pl.BlockSpec(memory_space=pltpu.VMEM), pl.BlockSpec(memory_space=pltpu.SMEM)
    return pl.pallas_call(
        functools.partial(prepare_kernel, group),
        in_specs=[smem, vmem, vmem],
        out_specs=[vmem] * 6 + [smem],
        out_shape=[
            wide(frames // 2, 4 * chans, 2 * chans),
            wide(frames // 2, 4 * chans, 2 * chans),
            wide(3 * (group + 2) * chans, group * chans),
            wide(3 * (group + 2) * chans, group * chans),
            wide(chans, 3 * chans),
            wide(9 * chans, chans),
            jax.ShapeDtypeStruct((3, frames), jnp.float32),
        ],
        compiler_params=pltpu.CompilerParams(vmem_limit_bytes=24 * MIB),
        cost_estimate=pl.CostEstimate(flops=0, bytes_accessed=4 << 20, transcendentals=0),
    )(lengths, temporal, spatial)


def row_shifts(block, rows):
    index = lax.broadcasted_iota(jnp.int32, block.shape, 0)
    above = jnp.where(index == 0, 0.0, pltpu.roll(block, 1, 0))
    below = jnp.where(index == rows - 1, 0.0, pltpu.roll(block, rows - 1, 0))
    return above.astype(jnp.bfloat16), below.astype(jnp.bfloat16)


def lanes(parts):
    return parts[0] if len(parts) == 1 else jnp.concatenate(parts, axis=1)


def forward_kernel(group, width, lag, *refs):
    now, before = refs[:group], refs[group : 2 * group]
    left, left_before, right, right_before, temporal, spatial, slope, turned, held = refs[2 * group :]
    step = pl.program_id(1)
    rows, chans = slope.shape[2], slope.shape[3]
    sources = []
    for e in range(group):
        line = []
        for ours, l_ref, r_ref in ((before[e], left_before, right_before), (now[e], left, right)):
            for frame in range(2):
                tile = ours[0, frame]
                if e == 0:
                    tile = jnp.where(step == 0, l_ref[0, frame], tile)
                if e == group - 1:
                    tile = jnp.where(step * group + e == width + 1, r_ref[0, frame], tile)
                line.append(tile)
                if ours is now[e]:
                    turned[e, frame] = tile.T
        sources.append(lanes(line))
    mixed = jnp.dot(
        jnp.concatenate(sources, axis=0), temporal[0], preferred_element_type=jnp.float32
    ).astype(jnp.bfloat16)
    for e in range(group):
        value = mixed[e * rows : (e + 1) * rows]
        above, below = row_shifts(value.astype(jnp.float32), rows)
        for frame in range(2):
            at = slice(frame * chans, (frame + 1) * chans)
            held[step * group + e, frame] = lanes([above[:, at], value[:, at], below[:, at]])

    @pl.when(step >= lag)
    def _():
        base = (step - lag) * group
        source = lanes([held[base + k].reshape(2 * rows, 3 * chans) for k in range(group + 2)])
        pre = jnp.dot(source, spatial[...], preferred_element_type=jnp.float32)
        sig = jax.nn.sigmoid(pre)
        value = sig * (1.0 + pre * (1.0 - sig))
        for e in range(group):
            slope[e] = value[:, e * chans : (e + 1) * chans].reshape(2, rows, chans)


def forward(video, left, right, temporal, spatial, group):
    width, frames, rows, chans = video.shape
    lag = 2 // group
    steps = (width + 2) // group

    def own(e, back):
        return pl.BlockSpec(
            (1, 2, rows, chans),
            lambda p, j: (
                jnp.clip(j * group + e - 1, 0, width - 1),
                jnp.maximum(p - back, 0),
                0,
                0,
            ),
        )

    def edge(back):
        return pl.BlockSpec((1, 2, rows, chans), lambda p, j: (0, jnp.maximum(p - back, 0), 0, 0))

    out = pl.BlockSpec((group, 2, rows, chans), lambda p, j: (jnp.maximum(j - lag, 0), p, 0, 0))
    pixels = width * frames * rows
    return pl.pallas_call(
        functools.partial(forward_kernel, group, width, lag),
        grid=(frames // 2, steps),
        in_specs=[own(e, 0) for e in range(group)]
        + [own(e, 1) for e in range(group)]
        + [
            edge(0),
            edge(1),
            edge(0),
            edge(1),
            pl.BlockSpec((1, 4 * chans, 2 * chans), lambda p, j: (p, 0, 0)),
            pl.BlockSpec(spatial.shape, lambda p, j: (0, 0)),
        ],
        out_specs=[out, pl.BlockSpec((group, 2, chans, rows), lambda p, j: (j, p, 0, 0))],
        out_shape=[
            jax.ShapeDtypeStruct((width, frames, rows, chans), jnp.float32),
            jax.ShapeDtypeStruct((width + 2, frames, chans, rows), jnp.bfloat16),
        ],
        scratch_shapes=[pltpu.VMEM((width + 2, 2, rows, 3 * chans), jnp.bfloat16)],
        compiler_params=pltpu.CompilerParams(vmem_limit_bytes=60 * MIB),
        cost_estimate=pl.CostEstimate(
            flops=pixels * chans * chans * 2 * 24 * 5,
            bytes_accessed=pixels * chans * 14,
            transcendentals=pixels * chans,
        ),
    )(*([video] * (2 * group)), left, left, right, right, temporal, spatial)


def moments_kernel(group, groups, places, edges, scale, masks, *refs):
    count = len(groups)
    grads, refs = refs[0], refs[1:]
    slopes, refs = refs[:count], refs[count:]
    now, before, refs = refs[: len(places)], refs[len(places) : 2 * len(places)], refs[2 * len(places) :]
    temporal, spatial, refs = refs[0], refs[1], refs[2:]
    total, refs = refs[-1], refs[:-1]
    if edges:
        head, tail, refs, earlier = refs[-2], refs[-1], refs[:-2], None
    else:
        earlier, refs = refs[0], refs[1:]
    deltas, sums = refs[:count], refs[count]
    pair = pl.program_id(0)
    bands, band = grads.shape[1], grads.shape[4]
    rows, chans = slopes[0].shape[2], slopes[0].shape[3]

    @pl.when(pair == 0)
    def _():
        total[...] = jnp.zeros_like(total)

    parts = [(n, frame) for frame in range(2) for n in range(count)]
    triples = []
    for n, frame in parts:
        line = []
        for e in range(group):
            for b in range(bands):
                at = slice(b * band, (b + 1) * band)
                value = grads[0, b, n * group + e, frame].astype(jnp.float32)
                deltas[n][e, frame, at] = (value * slopes[n][e, frame, at]).astype(jnp.bfloat16)
            value = deltas[n][e, frame]
            above, below = row_shifts(value.astype(jnp.float32), rows)
            line += [below, value, above]
        triples.append(lanes(line))
    right = jnp.concatenate(triples, axis=0)
    if edges:
        head[0] = deltas[0][0]
        tail[0] = deltas[-1][group - 1]

    def add(lag, left, right):
        total[lag] += jnp.dot(left, right, preferred_element_type=jnp.float32)

    def turned(refs, n, frame):
        first = groups[n] * group
        return jnp.concatenate(
            [
                refs[places.index(c // group)][c % group, frame]
                for c in range(first, first + group + 2)
            ],
            axis=0,
        )

    add(0, lanes([turned(now, n, frame) for n, frame in parts]), right)
    rest = count * rows
    for lag, frame, source, other in (
        (1, 0, before, 1),
        (1, 1, now, 0),
        (2, 0, before, 0),
        (2, 1, before, 1),
    ):

        @pl.when(masks[lag, 2 * pair + frame] > 0)
        def _():
            left = lanes([turned(source, n, other) for n in range(count)])
            add(lag, left, right[frame * rest : (frame + 1) * rest])

    @pl.when(pair == pl.num_programs(0) - 1)
    def _():
        lines = []
        for lag in range(3):
            line = []
            for a in range(3):
                for b in range(3):
                    line.append(
                        sum(
                            total[
                                lag,
                                (j + b) * chans : (j + b + 1) * chans,
                                (j * 3 + a) * chans : (j * 3 + a + 1) * chans,
                            ]
                            for j in range(group)
                        )
                    )
            lines.append(lanes(line))
        moments = jnp.concatenate(lines, axis=0)
        high = moments.astype(jnp.bfloat16)
        low = (moments - high.astype(jnp.float32)).astype(jnp.bfloat16)

        def product(left, right):
            return jnp.dot(left, right, preferred_element_type=jnp.float32)

        spatial_sum = product(temporal[...], high) + product(temporal[...], low)
        temporal_sum = product(high, spatial[...]) + product(low, spatial[...])
        for k in range(3):
            value = temporal_sum[k * chans : (k + 1) * chans] * scale
            sums[k] = value if earlier is None else earlier[k] + value
        for k in range(9):
            value = spatial_sum[:, k * chans : (k + 1) * chans] * scale
            sums[3 + k] = value if earlier is None else earlier[3 + k] + value


def moments(received, slope, turned, masks, temporal, spatial, earlier, groups, group):
    edges = earlier is None
    frames, rows, chans = slope.shape[1:]
    bands, band = received.shape[1], received.shape[4]
    count = len(groups)
    places = sorted({n + k for n in groups for k in range(2 // group + 1)})
    pixels = count * group * frames * rows
    scale = float(frames * rows * slope.shape[0] * lax.axis_size(MESH_AXES)) ** (-0.5)

    def own(n):
        return pl.BlockSpec((group, 2, rows, chans), lambda p, m: (n, p, 0, 0))

    def columns(n, back):
        return pl.BlockSpec(
            (group, 2, chans, rows), lambda p, m: (n, jnp.maximum(p - back, 0), 0, 0)
        )

    def whole(shape):
        return pl.BlockSpec(shape, lambda p, m: (0,) * len(shape))

    edge = pl.BlockSpec((1, 2, rows, chans), lambda p, m: (0, p, 0, 0))
    edge_shape = jax.ShapeDtypeStruct((1, frames, rows, chans), jnp.bfloat16)
    sums_shape = (12, chans, chans)
    outs = pl.pallas_call(
        functools.partial(moments_kernel, group, groups, places, edges, scale),
        grid_spec=pltpu.PrefetchScalarGridSpec(
            num_scalar_prefetch=1,
            grid=(frames // 2,),
            in_specs=[
                pl.BlockSpec(
                    (1, bands, count * group, 2, band, chans), lambda p, m: (p, 0, 0, 0, 0, 0)
                )
            ]
            + [own(n) for n in groups]
            + [columns(n, 0) for n in places]
            + [columns(n, 1) for n in places]
            + [whole(temporal.shape), whole(spatial.shape)]
            + ([] if edges else [whole(sums_shape)]),
            out_specs=[own(0) for _ in groups]
            + [whole(sums_shape)]
            + ([edge, edge] if edges else []),
            scratch_shapes=[
                pltpu.VMEM((3, (group + 2) * chans, group * 3 * chans), jnp.float32),
            ],
        ),
        out_shape=[jax.ShapeDtypeStruct((group, frames, rows, chans), jnp.bfloat16)] * count
        + [jax.ShapeDtypeStruct(sums_shape, jnp.float32)]
        + ([edge_shape, edge_shape] if edges else []),
        compiler_params=pltpu.CompilerParams(vmem_limit_bytes=60 * MIB),
        cost_estimate=pl.CostEstimate(
            flops=pixels * chans * chans * 2 * 30,
            bytes_accessed=pixels * chans * 20,
            transcendentals=0,
        ),
    )(
        masks,
        received,
        *([slope] * count),
        *([turned] * (2 * len(places))),
        temporal,
        spatial,
        *([] if edges else [earlier]),
    )
    return outs[:count], outs[count], outs[count + 1 :]


def backward_kernel(group, sources, *refs):
    spatial, temporal = refs[len(sources) : len(sources) + 2]
    out, later = refs[-2:]
    cols, rows, chans = out.shape[0], out.shape[2], out.shape[3]

    @pl.when(pl.program_id(0) == 0)
    def _():
        later[...] = jnp.zeros_like(later)

    triples = []
    for ref, col in zip(refs, sources):
        lines = []
        for frame in range(2):
            value = ref[col, frame]
            above, below = row_shifts(value.astype(jnp.float32), rows)
            lines.append(lanes([below, value, above]))
        triples.append(jnp.concatenate(lines, axis=0))
    grad = []
    for base in range(0, cols, group):
        source = lanes(triples[base : base + group + 2])
        back = jnp.dot(source, spatial[...], preferred_element_type=jnp.float32)
        back = back.astype(jnp.bfloat16)
        for e in range(group):
            at = slice(e * chans, (e + 1) * chans)
            grad.append(lanes([back[f * rows : (f + 1) * rows, at] for f in range(2)]))
    grad = jnp.concatenate(grad, axis=0)
    value = jnp.dot(
        lanes([grad, later[...]]), temporal[0], preferred_element_type=jnp.float32
    ).astype(jnp.bfloat16)
    later[...] = grad
    for col in range(cols):
        for frame in range(2):
            out[col, frame] = value[
                col * rows : (col + 1) * rows, frame * chans : (frame + 1) * chans
            ]


def backward(deltas, left, right, spatial, temporal, filled, first, cols):
    group, frames, rows, chans = deltas[0].shape
    width = group * len(deltas)
    filled = [] if filled is None else [filled]
    ext = [(left, 0)] + [(d, e) for d in deltas for e in range(group)] + [(right, 0)]
    ext = ext[first : first + cols + 2]
    part = first // cols
    last = frames // 2 - 1
    pixels = cols * frames * rows
    block = pl.BlockSpec((cols, 2, rows, chans), lambda p: (part, last - p, 0, 0))
    return pl.pallas_call(
        functools.partial(backward_kernel, group, [0] * len(ext)),
        grid=(frames // 2,),
        in_specs=[
            pl.BlockSpec(
                (1, 2, rows, chans), functools.partial(lambda e, p: (e, last - p, 0, 0), e)
            )
            for _, e in ext
        ]
        + [
            pl.BlockSpec(spatial.shape, lambda p: (0, 0)),
            pl.BlockSpec((1, 4 * chans, 2 * chans), lambda p: (last - p, 0, 0)),
        ]
        + [pl.BlockSpec(memory_space=pl.ANY)] * len(filled),
        out_specs=block,
        out_shape=jax.ShapeDtypeStruct((width, frames, rows, chans), jnp.bfloat16),
        input_output_aliases={len(ext) + 2: 0} if filled else {},
        scratch_shapes=[pltpu.VMEM((cols * rows, 2 * chans), jnp.bfloat16)],
        compiler_params=pltpu.CompilerParams(vmem_limit_bytes=60 * MIB),
        cost_estimate=pl.CostEstimate(
            flops=pixels * chans * chans * 2 * 24,
            bytes_accessed=pixels * chans * 6,
            transcendentals=0,
        ),
    )(*[array for array, _ in ext], spatial, temporal, *filled)


def exchanged(axis, parts):
    count = lax.axis_size(axis)
    return [
        lax.ppermute(parts(s), axis, [(i, i ^ s) for i in range(count)]) for s in range(1, count)
    ]


def sum_over_devices(local, works, state):
    def pieces(value, axis):
        me = lax.axis_index(axis)
        blocks = value.reshape(lax.axis_size(axis), -1, value.shape[-1])
        return lambda s: lax.dynamic_index_in_dim(blocks, me ^ s, 0, keepdims=False)

    def spread(parts, axis):
        order = jnp.arange(len(parts), dtype=jnp.int32) ^ lax.axis_index(axis)
        return jnp.take(jnp.stack(parts), order, axis=0).reshape(-1, parts[0].shape[-1])

    def beside(value, got, work, state):
        value, state = lax.optimization_barrier((value, state))
        got = got(value)
        state = work(state)
        got, state = lax.optimization_barrier((got, state))
        return value, got, state

    pick = pieces(local, "width")
    value = functools.reduce(jnp.add, exchanged("width", pick), pick(0))
    value, got, state = beside(
        value, lambda v: exchanged("height", pieces(v, "height")), works[0], state
    )
    value = functools.reduce(jnp.add, got, pieces(value, "height")(0))
    value, got, state = beside(value, lambda v: exchanged("tm", lambda s: v), works[1], state)
    value = functools.reduce(jnp.add, got, value)
    value, got, state = beside(value, lambda v: exchanged("height", lambda s: v), works[2], state)
    value = spread([value] + got, "height")
    return spread([value] + exchanged("width", lambda s: value), "width"), state


def shards(video, out_grad, lengths, temporal_weight, spatial_weight):
    clip = video[0]
    width, frames, rows, chans = clip.shape
    n_tm = lax.axis_size("tm")
    n_height = lax.axis_size("height")
    frames_dev, rows_dev = out_grad.shape[2], out_grad.shape[3]
    assert frames_dev == 2
    group = 2 if width % 2 == 0 else 1
    pairs = frames // 2

    left, right = column_neighbours(clip[:1], clip[width - 1 :])
    blocks = out_grad[0].reshape(n_tm * n_height, width, frames_dev, rows_dev, chans)

    def to_columns(part):
        got = lax.all_to_all(part, ("tm", "height"), split_axis=0, concat_axis=0, tiled=True)
        return got.reshape(n_tm, n_height, *part.shape[1:])

    early, later = list(range(width // group)), []
    if len(early) >= 4:
        later = [early.pop(-2)]
        cut = later[0] * group
        first = jnp.concatenate([blocks[:, :cut], blocks[:, cut + group :]], axis=1)
    else:
        first = blocks
    received = to_columns(first)

    temporal_mix, temporal_back, spatial_mix, spatial_back, *weights, masks = prepare(
        lengths, temporal_weight, spatial_weight, frames, group
    )
    slope, turned = forward(clip, left, right, temporal_mix, spatial_mix, group)
    if later:
        blocks, slope, turned = lax.optimization_barrier((blocks, slope, turned))
        second = blocks[:, cut : cut + group]
        second, received, slope, turned = lax.optimization_barrier(
            (second, received, slope, turned)
        )
        second = to_columns(second)

    weights = (slope, turned, masks, *weights)
    def edge_delta(col, place):
        grads = received[:, :, place].transpose(0, 2, 1, 3, 4).reshape(1, frames, rows, chans)
        return (grads.astype(jnp.float32) * slope[col][None]).astype(jnp.bfloat16)

    head, tail = edge_delta(0, 0), edge_delta(width - 1, received.shape[2] - 1)
    received, head, tail = lax.optimization_barrier((received, head, tail))
    delta_left, delta_right = column_neighbours(head, tail)
    deltas, local, _ = moments(received, *weights, None, early, group)
    if later:
        more, local, _ = moments(second, *weights, local, later, group)
        deltas = deltas[: later[0]] + more + deltas[later[0] :]
    local, deltas, delta_left, delta_right = lax.optimization_barrier(
        (local, deltas, delta_left, delta_right)
    )

    parts = [(0, width), None, None]
    if len(deltas) >= 4:
        half = width // 2
        parts = [(0, half), (half, half), None]

    def one_part(part, state):
        if part is None:
            return state
        operands, filled = state
        return operands, backward(*operands, spatial_back, temporal_back, filled, *part)

    sums, (_, video_grad) = sum_over_devices(
        local.reshape(-1, chans),
        [functools.partial(one_part, part) for part in parts],
        ((deltas, delta_left, delta_right), None),
    )
    sums = sums.reshape(12, chans, chans)
    temporal_grad, spatial_grad = sums[:3], sums[3:].reshape(3, 3, chans, chans)
    return video_grad[None], temporal_grad, spatial_grad


def solution(mesh):
    placed = (
        P("width", ("tm", "height"), None, None, None),
        P("width", None, "tm", "height", None),
        P(),
        P(),
        P(),
    )
    return jax.shard_map(
        shards,
        mesh=mesh,
        in_specs=placed,
        out_specs=(P("width", ("tm", "height"), None, None, None), P(), P()),
        check_vma=False,
    )
```

```python
import functools

import jax
import jax.numpy as jnp
from jax import lax
from jax.experimental import pallas as pl
from jax.experimental.pallas import tpu as pltpu
from jax.sharding import PartitionSpec as P

MESH_AXES = ("tm", "height", "width")
MIB = 1024 * 1024


def column_neighbours(first, last):
    n_tm, n_height, n_width = (lax.axis_size(axis) for axis in MESH_AXES)
    blocks = n_tm * n_height
    place = [(pos % blocks) * n_width + pos // blocks for pos in range(blocks * n_width)]
    pairs = list(zip(place[:-1], place[1:]))
    left = lax.ppermute(last, MESH_AXES, pairs)
    right = lax.ppermute(first, MESH_AXES, [(b, a) for a, b in pairs])
    return left, right


def prepare_kernel(group, lengths, temporal, spatial, *outs):
    mix, back, pre, grad, temporal_turned, spatial_turned, masks = outs
    frames, chans = masks.shape[1], temporal.shape[1]
    end, spans = jnp.int32(0), []
    for n in range(lengths.shape[0]):
        spans.append((end, end + lengths[n]))
        end = end + lengths[n]
    keep = []
    for frame in range(frames):
        first = jnp.int32(0)
        for start, stop in spans:
            first = first + jnp.where((frame >= start) & (frame < stop), start, 0)
        keep.append([jnp.where(frame - lag >= first, 1.0, 0.0) for lag in range(3)])
    for lag in range(3):
        for frame in range(frames):
            masks[lag, frame] = keep[frame][lag]

    zero = jnp.zeros((chans, chans), jnp.bfloat16)
    turned = [temporal[k].T for k in range(3)]
    for i in range(4):
        for j in range(2):
            at = (slice(i * chans, (i + 1) * chans), slice(j * chans, (j + 1) * chans))
            for p in range(frames // 2):
                k, frame = 2 + j - i, 2 * p + j
                value = zero
                if 0 <= k < 3:
                    value = jnp.where(keep[frame][k] > 0, temporal[k], zero)
                mix[(p, *at)] = value
                k, frame = i - j, 2 * p + i
                value = zero
                if 0 <= k < 3 and frame < frames:
                    value = jnp.where(keep[frame][k] > 0, turned[k], zero)
                back[(p, *at)] = value
    for k in range(3):
        temporal_turned[:, k * chans : (k + 1) * chans] = turned[k]
    for a in range(3):
        for b in range(3):
            value = spatial[a, b].T
            n = 3 * a + b
            spatial_turned[n * chans : (n + 1) * chans] = value
            for j in range(group):
                at = slice(j * chans, (j + 1) * chans)
                i = 3 * (b + j) + a
                pre[i * chans : (i + 1) * chans, at] = spatial[a, b]
                i = 3 * (j + 2 - b) + a
                grad[i * chans : (i + 1) * chans, at] = value
    for j in range(group):
        for i in range(group + 2):
            if not 0 <= i - j < 3:
                at = (slice(3 * i * chans, 3 * (i + 1) * chans), slice(j * chans, (j + 1) * chans))
                pre[at] = jnp.zeros((3 * chans, chans), jnp.bfloat16)
                grad[at] = jnp.zeros((3 * chans, chans), jnp.bfloat16)


def prepare(lengths, temporal, spatial, frames, group):
    chans = temporal.shape[1]

    def wide(*shape):
        return jax.ShapeDtypeStruct(shape, jnp.bfloat16)

    vmem, smem = pl.BlockSpec(memory_space=pltpu.VMEM), pl.BlockSpec(memory_space=pltpu.SMEM)
    return pl.pallas_call(
        functools.partial(prepare_kernel, group),
        in_specs=[smem, vmem, vmem],
        out_specs=[vmem] * 6 + [smem],
        out_shape=[
            wide(frames // 2, 4 * chans, 2 * chans),
            wide(frames // 2, 4 * chans, 2 * chans),
            wide(3 * (group + 2) * chans, group * chans),
            wide(3 * (group + 2) * chans, group * chans),
            wide(chans, 3 * chans),
            wide(9 * chans, chans),
            jax.ShapeDtypeStruct((3, frames), jnp.float32),
        ],
        compiler_params=pltpu.CompilerParams(vmem_limit_bytes=24 * MIB),
        cost_estimate=pl.CostEstimate(flops=0, bytes_accessed=4 << 20, transcendentals=0),
    )(lengths, temporal, spatial)


def row_shifts(block, rows):
    index = lax.broadcasted_iota(jnp.int32, block.shape, 0)
    above = jnp.where(index == 0, 0.0, pltpu.roll(block, 1, 0))
    below = jnp.where(index == rows - 1, 0.0, pltpu.roll(block, rows - 1, 0))
    return above.astype(jnp.bfloat16), below.astype(jnp.bfloat16)


def lanes(parts):
    return parts[0] if len(parts) == 1 else jnp.concatenate(parts, axis=1)


def forward_kernel(group, width, lag, *refs):
    now, before = refs[:group], refs[group : 2 * group]
    left, left_before, right, right_before, temporal, spatial, slope, turned, held = refs[2 * group :]
    step = pl.program_id(1)
    rows, chans = slope.shape[2], slope.shape[3]
    sources = []
    for e in range(group):
        line = []
        for ours, l_ref, r_ref in ((before[e], left_before, right_before), (now[e], left, right)):
            for frame in range(2):
                tile = ours[0, frame]
                if e == 0:
                    tile = jnp.where(step == 0, l_ref[0, frame], tile)
                if e == group - 1:
                    tile = jnp.where(step * group + e == width + 1, r_ref[0, frame], tile)
                line.append(tile)
                if ours is now[e]:
                    turned[e, frame] = tile.T
        sources.append(lanes(line))
    mixed = jnp.dot(
        jnp.concatenate(sources, axis=0), temporal[0], preferred_element_type=jnp.float32
    ).astype(jnp.bfloat16)
    for e in range(group):
        value = mixed[e * rows : (e + 1) * rows]
        above, below = row_shifts(value.astype(jnp.float32), rows)
        for frame in range(2):
            at = slice(frame * chans, (frame + 1) * chans)
            held[step * group + e, frame] = lanes([above[:, at], value[:, at], below[:, at]])

    @pl.when(step >= lag)
    def _():
        base = (step - lag) * group
        source = lanes([held[base + k].reshape(2 * rows, 3 * chans) for k in range(group + 2)])
        pre = jnp.dot(source, spatial[...], preferred_element_type=jnp.float32)
        sig = jax.nn.sigmoid(pre)
        value = sig * (1.0 + pre * (1.0 - sig))
        for e in range(group):
            slope[e] = value[:, e * chans : (e + 1) * chans].reshape(2, rows, chans)


def forward(video, left, right, temporal, spatial, group):
    width, frames, rows, chans = video.shape
    lag = 2 // group
    steps = (width + 2) // group

    def own(e, back):
        return pl.BlockSpec(
            (1, 2, rows, chans),
            lambda p, j: (
                jnp.clip(j * group + e - 1, 0, width - 1),
                jnp.maximum(p - back, 0),
                0,
                0,
            ),
        )

    def edge(back):
        return pl.BlockSpec((1, 2, rows, chans), lambda p, j: (0, jnp.maximum(p - back, 0), 0, 0))

    out = pl.BlockSpec((group, 2, rows, chans), lambda p, j: (jnp.maximum(j - lag, 0), p, 0, 0))
    pixels = width * frames * rows
    return pl.pallas_call(
        functools.partial(forward_kernel, group, width, lag),
        grid=(frames // 2, steps),
        in_specs=[own(e, 0) for e in range(group)]
        + [own(e, 1) for e in range(group)]
        + [
            edge(0),
            edge(1),
            edge(0),
            edge(1),
            pl.BlockSpec((1, 4 * chans, 2 * chans), lambda p, j: (p, 0, 0)),
            pl.BlockSpec(spatial.shape, lambda p, j: (0, 0)),
        ],
        out_specs=[out, pl.BlockSpec((group, 2, chans, rows), lambda p, j: (j, p, 0, 0))],
        out_shape=[
            jax.ShapeDtypeStruct((width, frames, rows, chans), jnp.float32),
            jax.ShapeDtypeStruct((width + 2, frames, chans, rows), jnp.bfloat16),
        ],
        scratch_shapes=[pltpu.VMEM((width + 2, 2, rows, 3 * chans), jnp.bfloat16)],
        compiler_params=pltpu.CompilerParams(vmem_limit_bytes=60 * MIB),
        cost_estimate=pl.CostEstimate(
            flops=pixels * chans * chans * 2 * 24 * 5,
            bytes_accessed=pixels * chans * 14,
            transcendentals=pixels * chans,
        ),
    )(*([video] * (2 * group)), left, left, right, right, temporal, spatial)


def moments_kernel(group, groups, places, fresh, scale, masks, *refs):
    count = len(groups)
    grads, refs = refs[0], refs[1:]
    slopes, refs = refs[:count], refs[count:]
    now, before, refs = refs[: len(places)], refs[len(places) : 2 * len(places)], refs[2 * len(places) :]
    temporal, spatial, refs = refs[0], refs[1], refs[2:]
    total, refs = refs[-1], refs[:-1]
    earlier, refs = (None, refs) if fresh else (refs[0], refs[1:])
    deltas, sums = refs[:count], refs[count]
    pair = pl.program_id(0)
    bands, band = grads.shape[1], grads.shape[4]
    rows, chans = slopes[0].shape[2], slopes[0].shape[3]

    @pl.when(pair == 0)
    def _():
        total[...] = jnp.zeros_like(total)

    parts = [(n, frame) for frame in range(2) for n in range(count)]
    triples = []
    for n, frame in parts:
        line = []
        for e in range(group):
            for b in range(bands):
                at = slice(b * band, (b + 1) * band)
                value = grads[0, b, n * group + e, frame].astype(jnp.float32)
                deltas[n][e, frame, at] = (value * slopes[n][e, frame, at]).astype(jnp.bfloat16)
            value = deltas[n][e, frame]
            above, below = row_shifts(value.astype(jnp.float32), rows)
            line += [below, value, above]
        triples.append(lanes(line))
    right = jnp.concatenate(triples, axis=0)

    def add(lag, left, right):
        total[lag] += jnp.dot(left, right, preferred_element_type=jnp.float32)

    def turned(refs, n, frame):
        first = groups[n] * group
        return jnp.concatenate(
            [
                refs[places.index(c // group)][c % group, frame]
                for c in range(first, first + group + 2)
            ],
            axis=0,
        )

    add(0, lanes([turned(now, n, frame) for n, frame in parts]), right)
    rest = count * rows
    for lag, frame, source, other in (
        (1, 0, before, 1),
        (1, 1, now, 0),
        (2, 0, before, 0),
        (2, 1, before, 1),
    ):

        @pl.when(masks[lag, 2 * pair + frame] > 0)
        def _():
            left = lanes([turned(source, n, other) for n in range(count)])
            add(lag, left, right[frame * rest : (frame + 1) * rest])

    @pl.when(pair == pl.num_programs(0) - 1)
    def _():
        lines = []
        for lag in range(3):
            line = []
            for a in range(3):
                for b in range(3):
                    line.append(
                        sum(
                            total[
                                lag,
                                (j + b) * chans : (j + b + 1) * chans,
                                (j * 3 + a) * chans : (j * 3 + a + 1) * chans,
                            ]
                            for j in range(group)
                        )
                    )
            lines.append(lanes(line))
        moments = jnp.concatenate(lines, axis=0)
        high = moments.astype(jnp.bfloat16)
        low = (moments - high.astype(jnp.float32)).astype(jnp.bfloat16)

        def product(left, right):
            return jnp.dot(left, right, preferred_element_type=jnp.float32)

        spatial_sum = product(temporal[...], high) + product(temporal[...], low)
        temporal_sum = product(high, spatial[...]) + product(low, spatial[...])
        for k in range(3):
            value = temporal_sum[k * chans : (k + 1) * chans] * scale
            sums[k] = value if earlier is None else earlier[k] + value
        for k in range(9):
            value = spatial_sum[:, k * chans : (k + 1) * chans] * scale
            sums[3 + k] = value if earlier is None else earlier[3 + k] + value


def moments(received, slope, turned, masks, temporal, spatial, earlier, groups, group):
    fresh = earlier is None
    frames, rows, chans = slope.shape[1:]
    bands, band = received.shape[1], received.shape[4]
    count = len(groups)
    places = sorted({n + k for n in groups for k in range(2 // group + 1)})
    pixels = count * group * frames * rows
    scale = float(frames * rows * slope.shape[0] * lax.axis_size(MESH_AXES)) ** (-0.5)

    def own(n):
        return pl.BlockSpec((group, 2, rows, chans), lambda p, m: (n, p, 0, 0))

    def columns(n, back):
        return pl.BlockSpec(
            (group, 2, chans, rows), lambda p, m: (n, jnp.maximum(p - back, 0), 0, 0)
        )

    def whole(shape):
        return pl.BlockSpec(shape, lambda p, m: (0,) * len(shape))

    sums_shape = (12, chans, chans)
    *deltas, sums = pl.pallas_call(
        functools.partial(moments_kernel, group, groups, places, fresh, scale),
        grid_spec=pltpu.PrefetchScalarGridSpec(
            num_scalar_prefetch=1,
            grid=(frames // 2,),
            in_specs=[
                pl.BlockSpec(
                    (1, bands, count * group, 2, band, chans), lambda p, m: (p, 0, 0, 0, 0, 0)
                )
            ]
            + [own(n) for n in groups]
            + [columns(n, 0) for n in places]
            + [columns(n, 1) for n in places]
            + [whole(temporal.shape), whole(spatial.shape)]
            + ([] if fresh else [whole(sums_shape)]),
            out_specs=[own(0) for _ in groups] + [whole(sums_shape)],
            scratch_shapes=[
                pltpu.VMEM((3, (group + 2) * chans, group * 3 * chans), jnp.float32),
            ],
        ),
        out_shape=[jax.ShapeDtypeStruct((group, frames, rows, chans), jnp.bfloat16)] * count
        + [jax.ShapeDtypeStruct(sums_shape, jnp.float32)],
        compiler_params=pltpu.CompilerParams(vmem_limit_bytes=60 * MIB),
        cost_estimate=pl.CostEstimate(
            flops=pixels * chans * chans * 2 * 30,
            bytes_accessed=pixels * chans * 20,
            transcendentals=0,
        ),
    )(
        masks,
        received,
        *([slope] * count),
        *([turned] * (2 * len(places))),
        temporal,
        spatial,
        *([] if fresh else [earlier]),
    )
    return deltas, sums


def backward_kernel(group, sources, *refs):
    spatial, temporal = refs[len(sources) : len(sources) + 2]
    out, later = refs[-2:]
    cols, rows, chans = out.shape[0], out.shape[2], out.shape[3]

    @pl.when(pl.program_id(0) == 0)
    def _():
        later[...] = jnp.zeros_like(later)

    triples = []
    for ref, col in zip(refs, sources):
        lines = []
        for frame in range(2):
            value = ref[col, frame]
            above, below = row_shifts(value.astype(jnp.float32), rows)
            lines.append(lanes([below, value, above]))
        triples.append(jnp.concatenate(lines, axis=0))
    grad = []
    for base in range(0, cols, group):
        source = lanes(triples[base : base + group + 2])
        back = jnp.dot(source, spatial[...], preferred_element_type=jnp.float32)
        back = back.astype(jnp.bfloat16)
        for e in range(group):
            at = slice(e * chans, (e + 1) * chans)
            grad.append(lanes([back[f * rows : (f + 1) * rows, at] for f in range(2)]))
    grad = jnp.concatenate(grad, axis=0)
    value = jnp.dot(
        lanes([grad, later[...]]), temporal[0], preferred_element_type=jnp.float32
    ).astype(jnp.bfloat16)
    later[...] = grad
    for col in range(cols):
        for frame in range(2):
            out[col, frame] = value[
                col * rows : (col + 1) * rows, frame * chans : (frame + 1) * chans
            ]


def backward(deltas, left, right, spatial, temporal, filled, first, cols):
    group, frames, rows, chans = deltas[0].shape
    width = group * len(deltas)
    filled = [] if filled is None else [filled]
    ext = [(left, 0)] + [(d, e) for d in deltas for e in range(group)] + [(right, 0)]
    ext = ext[first : first + cols + 2]
    part = first // cols
    last = frames // 2 - 1
    pixels = cols * frames * rows
    block = pl.BlockSpec((cols, 2, rows, chans), lambda p: (part, last - p, 0, 0))
    return pl.pallas_call(
        functools.partial(backward_kernel, group, [0] * len(ext)),
        grid=(frames // 2,),
        in_specs=[
            pl.BlockSpec(
                (1, 2, rows, chans), functools.partial(lambda e, p: (e, last - p, 0, 0), e)
            )
            for _, e in ext
        ]
        + [
            pl.BlockSpec(spatial.shape, lambda p: (0, 0)),
            pl.BlockSpec((1, 4 * chans, 2 * chans), lambda p: (last - p, 0, 0)),
        ]
        + [pl.BlockSpec(memory_space=pl.ANY)] * len(filled),
        out_specs=block,
        out_shape=jax.ShapeDtypeStruct((width, frames, rows, chans), jnp.bfloat16),
        input_output_aliases={len(ext) + 2: 0} if filled else {},
        scratch_shapes=[pltpu.VMEM((cols * rows, 2 * chans), jnp.bfloat16)],
        compiler_params=pltpu.CompilerParams(vmem_limit_bytes=60 * MIB),
        cost_estimate=pl.CostEstimate(
            flops=pixels * chans * chans * 2 * 24,
            bytes_accessed=pixels * chans * 6,
            transcendentals=0,
        ),
    )(*[array for array, _ in ext], spatial, temporal, *filled)


def exchanged(axis, parts):
    count = lax.axis_size(axis)
    return [
        lax.ppermute(parts(s), axis, [(i, i ^ s) for i in range(count)]) for s in range(1, count)
    ]


def sum_over_devices(local, works, state):
    def pieces(value, axis):
        me = lax.axis_index(axis)
        blocks = value.reshape(lax.axis_size(axis), -1, value.shape[-1])
        return lambda s: lax.dynamic_index_in_dim(blocks, me ^ s, 0, keepdims=False)

    def spread(parts, axis):
        order = jnp.arange(len(parts), dtype=jnp.int32) ^ lax.axis_index(axis)
        return jnp.take(jnp.stack(parts), order, axis=0).reshape(-1, parts[0].shape[-1])

    def beside(value, got, work, state):
        value, state = lax.optimization_barrier((value, state))
        got = got(value)
        state = work(state)
        got, state = lax.optimization_barrier((got, state))
        return value, got, state

    pick = pieces(local, "width")
    value = functools.reduce(jnp.add, exchanged("width", pick), pick(0))
    value, got, state = beside(
        value, lambda v: exchanged("height", pieces(v, "height")), works[0], state
    )
    value = functools.reduce(jnp.add, got, pieces(value, "height")(0))
    value, got, state = beside(value, lambda v: exchanged("tm", lambda s: v), works[1], state)
    value = functools.reduce(jnp.add, got, value)
    value, got, state = beside(value, lambda v: exchanged("height", lambda s: v), works[2], state)
    value = spread([value] + got, "height")
    return spread([value] + exchanged("width", lambda s: value), "width"), state


def shards(video, out_grad, lengths, temporal_weight, spatial_weight):
    clip = video[0]
    width, frames, rows, chans = clip.shape
    n_tm = lax.axis_size("tm")
    n_height = lax.axis_size("height")
    frames_dev, rows_dev = out_grad.shape[2], out_grad.shape[3]
    assert frames_dev == 2
    group = 2 if width % 2 == 0 else 1
    pairs = frames // 2

    left, right = column_neighbours(clip[:1], clip[width - 1 :])
    blocks = out_grad[0].reshape(n_tm * n_height, width, frames_dev, rows_dev, chans)

    def to_columns(part):
        got = lax.all_to_all(part, ("tm", "height"), split_axis=0, concat_axis=0, tiled=True)
        return got.reshape(n_tm, n_height, *part.shape[1:])

    count = width // group
    chunks = [list(range(count))]
    if count >= 4:
        chunks = [[0, count - 1], list(range(1, count - 1))]

    def outgoing(blocks, groups):
        if len(groups) == count:
            return blocks
        runs = [blocks[:, n * group : (n + 1) * group] for n in groups]
        return runs[0] if len(runs) == 1 else jnp.concatenate(runs, axis=1)

    received = to_columns(outgoing(blocks, chunks[0]))

    temporal_mix, temporal_back, spatial_mix, spatial_back, *weights, masks = prepare(
        lengths, temporal_weight, spatial_weight, frames, group
    )
    slope, turned = forward(clip, left, right, temporal_mix, spatial_mix, group)
    second = None
    if len(chunks) > 1:
        second = outgoing(blocks, chunks[1])
        second, received = lax.optimization_barrier((second, received))
        second = to_columns(second)
    weights = (slope, turned, masks, *weights)
    deltas, local = [None] * count, None

    def add(received, groups):
        some, total = moments(received, *weights, local, groups, group)
        for n, delta in zip(groups, some):
            deltas[n] = delta
        return total

    def edge_delta(received, col, place):
        grads = received[:, :, place].transpose(0, 2, 1, 3, 4).reshape(1, frames, rows, chans)
        return (grads.astype(jnp.float32) * slope[col][None]).astype(jnp.bfloat16)

    head = edge_delta(received, 0, 0)
    tail = edge_delta(received, width - 1, received.shape[2] - 1)
    received, head, tail = lax.optimization_barrier((received, head, tail))
    delta_left, delta_right = column_neighbours(head, tail)
    local = add(received, chunks[0])
    if second is not None:
        local = add(second, chunks[1])
    local, deltas, delta_left, delta_right = lax.optimization_barrier(
        (local, deltas, delta_left, delta_right)
    )

    parts = [(0, width), None, None]
    if len(deltas) >= 4:
        half = width // 2
        parts = [(0, half), (half, half), None]

    def one_part(part, state):
        if part is None:
            return state
        operands, filled = state
        return operands, backward(*operands, spatial_back, temporal_back, filled, *part)

    sums, (_, video_grad) = sum_over_devices(
        local.reshape(-1, chans),
        [functools.partial(one_part, part) for part in parts],
        ((deltas, delta_left, delta_right), None),
    )
    sums = sums.reshape(12, chans, chans)
    temporal_grad, spatial_grad = sums[:3], sums[3:].reshape(3, 3, chans, chans)
    return video_grad[None], temporal_grad, spatial_grad


def solution(mesh):
    placed = (
        P("width", ("tm", "height"), None, None, None),
        P("width", None, "tm", "height", None),
        P(),
        P(),
        P(),
    )
    return jax.shard_map(
        shards,
        mesh=mesh,
        in_specs=placed,
        out_specs=(P("width", ("tm", "height"), None, None, None), P(), P()),
        check_vma=False,
    )
```

```python
import functools

import jax
import jax.numpy as jnp
from jax import lax
from jax.experimental import pallas as pl
from jax.experimental.pallas import tpu as pltpu
from jax.sharding import PartitionSpec as P

MESH_AXES = ("tm", "height", "width")
MIB = 1024 * 1024


def column_neighbours(first, last):
    n_tm, n_height, n_width = (lax.axis_size(axis) for axis in MESH_AXES)
    blocks = n_tm * n_height
    place = [(pos % blocks) * n_width + pos // blocks for pos in range(blocks * n_width)]
    pairs = list(zip(place[:-1], place[1:]))
    left = lax.ppermute(last, MESH_AXES, pairs)
    right = lax.ppermute(first, MESH_AXES, [(b, a) for a, b in pairs])
    return left, right


def prepare_kernel(group, lengths, temporal, spatial, *outs):
    mix, back, pre, grad, temporal_turned, spatial_turned, masks = outs
    frames, chans = masks.shape[1], temporal.shape[1]
    end, spans = jnp.int32(0), []
    for n in range(lengths.shape[0]):
        spans.append((end, end + lengths[n]))
        end = end + lengths[n]
    keep = []
    for frame in range(frames):
        first = jnp.int32(0)
        for start, stop in spans:
            first = first + jnp.where((frame >= start) & (frame < stop), start, 0)
        keep.append([jnp.where(frame - lag >= first, 1.0, 0.0) for lag in range(3)])
    for lag in range(3):
        for frame in range(frames):
            masks[lag, frame] = keep[frame][lag]

    zero = jnp.zeros((chans, chans), jnp.bfloat16)
    turned = [temporal[k].T for k in range(3)]
    for i in range(4):
        for j in range(2):
            at = (slice(i * chans, (i + 1) * chans), slice(j * chans, (j + 1) * chans))
            for p in range(frames // 2):
                k, frame = 2 + j - i, 2 * p + j
                value = zero
                if 0 <= k < 3:
                    value = jnp.where(keep[frame][k] > 0, temporal[k], zero)
                mix[(p, *at)] = value
                k, frame = i - j, 2 * p + i
                value = zero
                if 0 <= k < 3 and frame < frames:
                    value = jnp.where(keep[frame][k] > 0, turned[k], zero)
                back[(p, *at)] = value
    for k in range(3):
        temporal_turned[:, k * chans : (k + 1) * chans] = turned[k]
    for a in range(3):
        for b in range(3):
            value = spatial[a, b].T
            n = 3 * a + b
            spatial_turned[n * chans : (n + 1) * chans] = value
            for j in range(group):
                at = slice(j * chans, (j + 1) * chans)
                i = 3 * (b + j) + a
                pre[i * chans : (i + 1) * chans, at] = spatial[a, b]
                i = 3 * (j + 2 - b) + a
                grad[i * chans : (i + 1) * chans, at] = value
    for j in range(group):
        for i in range(group + 2):
            if not 0 <= i - j < 3:
                at = (slice(3 * i * chans, 3 * (i + 1) * chans), slice(j * chans, (j + 1) * chans))
                pre[at] = jnp.zeros((3 * chans, chans), jnp.bfloat16)
                grad[at] = jnp.zeros((3 * chans, chans), jnp.bfloat16)


def prepare(lengths, temporal, spatial, frames, group):
    chans = temporal.shape[1]

    def wide(*shape):
        return jax.ShapeDtypeStruct(shape, jnp.bfloat16)

    vmem, smem = pl.BlockSpec(memory_space=pltpu.VMEM), pl.BlockSpec(memory_space=pltpu.SMEM)
    return pl.pallas_call(
        functools.partial(prepare_kernel, group),
        in_specs=[smem, vmem, vmem],
        out_specs=[vmem] * 6 + [smem],
        out_shape=[
            wide(frames // 2, 4 * chans, 2 * chans),
            wide(frames // 2, 4 * chans, 2 * chans),
            wide(3 * (group + 2) * chans, group * chans),
            wide(3 * (group + 2) * chans, group * chans),
            wide(chans, 3 * chans),
            wide(9 * chans, chans),
            jax.ShapeDtypeStruct((3, frames), jnp.float32),
        ],
        compiler_params=pltpu.CompilerParams(vmem_limit_bytes=24 * MIB),
        cost_estimate=pl.CostEstimate(flops=0, bytes_accessed=4 << 20, transcendentals=0),
    )(lengths, temporal, spatial)


def row_shifts(block, rows):
    index = lax.broadcasted_iota(jnp.int32, block.shape, 0)
    above = jnp.where(index == 0, 0.0, pltpu.roll(block, 1, 0))
    below = jnp.where(index == rows - 1, 0.0, pltpu.roll(block, rows - 1, 0))
    return above.astype(jnp.bfloat16), below.astype(jnp.bfloat16)


def lanes(parts):
    return parts[0] if len(parts) == 1 else jnp.concatenate(parts, axis=1)


def forward_kernel(group, now, before, left, left_before, right, right_before, *refs):
    temporal, spatial, slope, turned = refs
    width, rows, chans = slope.shape[0], slope.shape[2], slope.shape[3]
    columns = [(left_before.at[0], left.at[0])]
    columns += [(before.at[c], now.at[c]) for c in range(width)]
    columns += [(right_before.at[0], right.at[0])]
    triples = []
    for base in range(0, width + 2, group):
        sources = []
        for e in range(group):
            older, newer = columns[base + e]
            for frame in range(2):
                turned[base + e, frame] = newer[frame].T
            sources.append(lanes([ref[frame] for ref in (older, newer) for frame in range(2)]))
        mixed = jnp.dot(
            jnp.concatenate(sources, axis=0), temporal[0], preferred_element_type=jnp.float32
        ).astype(jnp.bfloat16)
        for e in range(group):
            lines = []
            for frame in range(2):
                value = mixed[e * rows : (e + 1) * rows, frame * chans : (frame + 1) * chans]
                above, below = row_shifts(value.astype(jnp.float32), rows)
                lines.append(lanes([above, value, below]))
            triples.append(jnp.concatenate(lines, axis=0))
    for base in range(0, width, group):
        source = lanes(triples[base : base + group + 2])
        pre = jnp.dot(source, spatial[...], preferred_element_type=jnp.float32)
        sig = jax.nn.sigmoid(pre)
        value = sig * (1.0 + pre * (1.0 - sig))
        for e in range(group):
            slope[base + e] = value[:, e * chans : (e + 1) * chans].reshape(2, rows, chans)


def forward(video, left, right, temporal, spatial, group):
    width, frames, rows, chans = video.shape

    def pair(cols, back):
        return pl.BlockSpec((cols, 2, rows, chans), lambda p: (0, jnp.maximum(p - back, 0), 0, 0))

    pixels = width * frames * rows
    return pl.pallas_call(
        functools.partial(forward_kernel, group),
        grid=(frames // 2,),
        in_specs=[
            pair(width, 0),
            pair(width, 1),
            pair(1, 0),
            pair(1, 1),
            pair(1, 0),
            pair(1, 1),
            pl.BlockSpec((1, 4 * chans, 2 * chans), lambda p: (p, 0, 0)),
            pl.BlockSpec(spatial.shape, lambda p: (0, 0)),
        ],
        out_specs=[
            pair(width, 0),
            pl.BlockSpec((width + 2, 2, chans, rows), lambda p: (0, p, 0, 0)),
        ],
        out_shape=[
            jax.ShapeDtypeStruct((width, frames, rows, chans), jnp.float32),
            jax.ShapeDtypeStruct((width + 2, frames, chans, rows), jnp.bfloat16),
        ],
        compiler_params=pltpu.CompilerParams(vmem_limit_bytes=60 * MIB),
        cost_estimate=pl.CostEstimate(
            flops=pixels * chans * chans * 2 * 24 * 5,
            bytes_accessed=pixels * chans * 14,
            transcendentals=pixels * chans,
        ),
    )(video, video, left, left, right, right, temporal, spatial)


def moments_kernel(group, groups, places, fresh, final, scale, masks, side, *refs):
    count = len(groups)
    grads, refs = refs[0], refs[1:]
    slopes, refs = refs[:count], refs[count:]
    now, before, refs = refs[: len(places)], refs[len(places) : 2 * len(places)], refs[2 * len(places) :]
    temporal, spatial, refs = refs[0], refs[1], refs[2:]
    total, ordered, refs = refs[-2], refs[-1], refs[:-2]
    earlier, refs = (None, refs) if fresh else (refs[0], refs[1:])
    deltas, sums = refs[:count], ordered if final else refs[count]
    pair = pl.program_id(0)
    bands, band = grads.shape[1], grads.shape[4]
    rows, chans = slopes[0].shape[2], slopes[0].shape[3]

    @pl.when(pair == 0)
    def _():
        total[...] = jnp.zeros_like(total)

    parts = [(n, frame) for frame in range(2) for n in range(count)]
    triples = []
    for n, frame in parts:
        line = []
        for e in range(group):
            for b in range(bands):
                at = slice(b * band, (b + 1) * band)
                value = grads[0, b, n * group + e, frame].astype(jnp.float32)
                deltas[n][e, frame, at] = (value * slopes[n][e, frame, at]).astype(jnp.bfloat16)
            value = deltas[n][e, frame]
            above, below = row_shifts(value.astype(jnp.float32), rows)
            line += [below, value, above]
        triples.append(lanes(line))
    right = jnp.concatenate(triples, axis=0)

    def add(lag, left, right):
        total[lag] += jnp.dot(left, right, preferred_element_type=jnp.float32)

    def turned(refs, n, frame):
        first = groups[n] * group
        return jnp.concatenate(
            [
                refs[places.index(c // group)][c % group, frame]
                for c in range(first, first + group + 2)
            ],
            axis=0,
        )

    add(0, lanes([turned(now, n, frame) for n, frame in parts]), right)
    rest = count * rows
    for lag, frame, source, other in (
        (1, 0, before, 1),
        (1, 1, now, 0),
        (2, 0, before, 0),
        (2, 1, before, 1),
    ):

        @pl.when(masks[lag, 2 * pair + frame] > 0)
        def _():
            left = lanes([turned(source, n, other) for n in range(count)])
            add(lag, left, right[frame * rest : (frame + 1) * rest])

    @pl.when(pair == pl.num_programs(0) - 1)
    def _():
        lines = []
        for lag in range(3):
            line = []
            for a in range(3):
                for b in range(3):
                    line.append(
                        sum(
                            total[
                                lag,
                                (j + b) * chans : (j + b + 1) * chans,
                                (j * 3 + a) * chans : (j * 3 + a + 1) * chans,
                            ]
                            for j in range(group)
                        )
                    )
            lines.append(lanes(line))
        moments = jnp.concatenate(lines, axis=0)
        high = moments.astype(jnp.bfloat16)
        low = (moments - high.astype(jnp.float32)).astype(jnp.bfloat16)

        def product(left, right):
            return jnp.dot(left, right, preferred_element_type=jnp.float32)

        spatial_sum = product(temporal[...], high) + product(temporal[...], low)
        temporal_sum = product(high, spatial[...]) + product(low, spatial[...])
        for k in range(3):
            value = temporal_sum[k * chans : (k + 1) * chans] * scale
            sums[k] = value if earlier is None else earlier[k] + value
        for k in range(9):
            value = spatial_sum[:, k * chans : (k + 1) * chans] * scale
            sums[3 + k] = value if earlier is None else earlier[3 + k] + value
        if final:
            half = ordered.shape[0] // 2
            refs[count][...] = ordered[pl.ds(half * side[0], half)]
            refs[count + 1][...] = ordered[pl.ds(half * (1 - side[0]), half)]


def moments(received, slope, turned, masks, temporal, spatial, earlier, groups, group, final):
    fresh = earlier is None
    frames, rows, chans = slope.shape[1:]
    bands, band = received.shape[1], received.shape[4]
    count = len(groups)
    places = sorted({n + k for n in groups for k in range(2 // group + 1)})
    pixels = count * group * frames * rows
    scale = float(frames * rows * slope.shape[0] * lax.axis_size(MESH_AXES)) ** (-0.5)

    def own(n):
        return pl.BlockSpec((group, 2, rows, chans), lambda p, *m: (n, p, 0, 0))

    def columns(n, back):
        return pl.BlockSpec(
            (group, 2, chans, rows), lambda p, *m: (n, jnp.maximum(p - back, 0), 0, 0)
        )

    def whole(shape):
        return pl.BlockSpec(shape, lambda p, *m: (0,) * len(shape))

    sums_shape = (12, chans, chans)
    outs = [(6, chans, chans)] * 2 if final else [sums_shape]
    side = lax.axis_index("width").astype(jnp.int32).reshape(1)
    results = pl.pallas_call(
        functools.partial(moments_kernel, group, groups, places, fresh, final, scale),
        grid_spec=pltpu.PrefetchScalarGridSpec(
            num_scalar_prefetch=2,
            grid=(frames // 2,),
            in_specs=[
                pl.BlockSpec(
                    (1, bands, count * group, 2, band, chans), lambda p, *m: (p, 0, 0, 0, 0, 0)
                )
            ]
            + [own(n) for n in groups]
            + [columns(n, 0) for n in places]
            + [columns(n, 1) for n in places]
            + [whole(temporal.shape), whole(spatial.shape)]
            + ([] if fresh else [whole(sums_shape)]),
            out_specs=[own(0) for _ in groups] + [whole(shape) for shape in outs],
            scratch_shapes=[
                pltpu.VMEM((3, (group + 2) * chans, group * 3 * chans), jnp.float32),
                pltpu.VMEM(sums_shape, jnp.float32),
            ],
        ),
        out_shape=[jax.ShapeDtypeStruct((group, frames, rows, chans), jnp.bfloat16)] * count
        + [jax.ShapeDtypeStruct(shape, jnp.float32) for shape in outs],
        compiler_params=pltpu.CompilerParams(vmem_limit_bytes=60 * MIB),
        cost_estimate=pl.CostEstimate(
            flops=pixels * chans * chans * 2 * 30,
            bytes_accessed=pixels * chans * 20,
            transcendentals=0,
        ),
    )(
        masks,
        side,
        received,
        *([slope] * count),
        *([turned] * (2 * len(places))),
        temporal,
        spatial,
        *([] if fresh else [earlier]),
    )
    return results[:count], results[count:] if final else results[count]


def backward_kernel(group, sources, *refs):
    spatial, temporal = refs[len(sources) : len(sources) + 2]
    out, later = refs[-2:]
    cols, rows, chans = out.shape[0], out.shape[2], out.shape[3]

    @pl.when(pl.program_id(0) == 0)
    def _():
        later[...] = jnp.zeros_like(later)

    triples = []
    for ref, col in zip(refs, sources):
        lines = []
        for frame in range(2):
            value = ref[col, frame]
            above, below = row_shifts(value.astype(jnp.float32), rows)
            lines.append(lanes([below, value, above]))
        triples.append(jnp.concatenate(lines, axis=0))
    grad = []
    for base in range(0, cols, group):
        source = lanes(triples[base : base + group + 2])
        back = jnp.dot(source, spatial[...], preferred_element_type=jnp.float32)
        back = back.astype(jnp.bfloat16)
        for e in range(group):
            at = slice(e * chans, (e + 1) * chans)
            grad.append(lanes([back[f * rows : (f + 1) * rows, at] for f in range(2)]))
    grad = jnp.concatenate(grad, axis=0)
    value = jnp.dot(
        lanes([grad, later[...]]), temporal[0], preferred_element_type=jnp.float32
    ).astype(jnp.bfloat16)
    later[...] = grad
    for col in range(cols):
        for frame in range(2):
            out[col, frame] = value[
                col * rows : (col + 1) * rows, frame * chans : (frame + 1) * chans
            ]


def backward(deltas, left, right, spatial, temporal, filled, first, cols):
    group, frames, rows, chans = deltas[0].shape
    width = group * len(deltas)
    filled = [] if filled is None else [filled]
    ext = [(left, 0)] + [(d, e) for d in deltas for e in range(group)] + [(right, 0)]
    ext = ext[first : first + cols + 2]
    part = first // cols
    last = frames // 2 - 1
    pixels = cols * frames * rows
    block = pl.BlockSpec((cols, 2, rows, chans), lambda p: (part, last - p, 0, 0))
    return pl.pallas_call(
        functools.partial(backward_kernel, group, [0] * len(ext)),
        grid=(frames // 2,),
        in_specs=[
            pl.BlockSpec(
                (1, 2, rows, chans), functools.partial(lambda e, p: (e, last - p, 0, 0), e)
            )
            for _, e in ext
        ]
        + [
            pl.BlockSpec(spatial.shape, lambda p: (0, 0)),
            pl.BlockSpec((1, 4 * chans, 2 * chans), lambda p: (last - p, 0, 0)),
        ]
        + [pl.BlockSpec(memory_space=pl.ANY)] * len(filled),
        out_specs=block,
        out_shape=jax.ShapeDtypeStruct((width, frames, rows, chans), jnp.bfloat16),
        input_output_aliases={len(ext) + 2: 0} if filled else {},
        scratch_shapes=[pltpu.VMEM((cols * rows, 2 * chans), jnp.bfloat16)],
        compiler_params=pltpu.CompilerParams(vmem_limit_bytes=60 * MIB),
        cost_estimate=pl.CostEstimate(
            flops=pixels * chans * chans * 2 * 24,
            bytes_accessed=pixels * chans * 6,
            transcendentals=0,
        ),
    )(*[array for array, _ in ext], spatial, temporal, *filled)


def exchanged(axis, parts):
    count = lax.axis_size(axis)
    return [
        lax.ppermute(parts(s), axis, [(i, i ^ s) for i in range(count)]) for s in range(1, count)
    ]


def sum_over_devices(local, works, state):
    def pieces(value, axis):
        me = lax.axis_index(axis)
        blocks = value.reshape(lax.axis_size(axis), -1, value.shape[-1])
        return lambda s: lax.dynamic_index_in_dim(blocks, me ^ s, 0, keepdims=False)

    def spread(parts, axis):
        order = jnp.arange(len(parts), dtype=jnp.int32) ^ lax.axis_index(axis)
        return jnp.take(jnp.stack(parts), order, axis=0).reshape(-1, parts[0].shape[-1])

    def beside(value, got, work, state):
        value, state = lax.optimization_barrier((value, state))
        got = got(value)
        state = work(state)
        got, state = lax.optimization_barrier((got, state))
        return value, got, state

    keep, send = local
    value = keep + exchanged("width", lambda s: send)[0]
    value, got, state = beside(
        value, lambda v: exchanged("height", pieces(v, "height")), works[0], state
    )
    value = functools.reduce(jnp.add, got, pieces(value, "height")(0))
    value, got, state = beside(value, lambda v: exchanged("tm", lambda s: v), works[1], state)
    value = functools.reduce(jnp.add, got, value)
    value, got, state = beside(value, lambda v: exchanged("height", lambda s: v), works[2], state)
    value = spread([value] + got, "height")
    (other,) = exchanged("width", lambda s: value)
    swap = lax.axis_index("width") == 1
    return [jnp.where(swap, other, value), jnp.where(swap, value, other)], state


def shards(video, out_grad, lengths, temporal_weight, spatial_weight):
    clip = video[0]
    width, frames, rows, chans = clip.shape
    n_tm = lax.axis_size("tm")
    n_height = lax.axis_size("height")
    frames_dev, rows_dev = out_grad.shape[2], out_grad.shape[3]
    assert frames_dev == 2
    group = 2 if width % 2 == 0 else 1
    pairs = frames // 2

    left, right = column_neighbours(clip[:1], clip[width - 1 :])
    blocks = out_grad[0].reshape(n_tm * n_height, width, frames_dev, rows_dev, chans)

    def to_columns(part):
        got = lax.all_to_all(part, ("tm", "height"), split_axis=0, concat_axis=0, tiled=True)
        return got.reshape(n_tm, n_height, *part.shape[1:])

    count = width // group
    chunks = [list(range(count))]
    if count >= 4:
        chunks = [[0, count - 1], list(range(1, count - 1))]

    def outgoing(blocks, groups):
        if len(groups) == count:
            return blocks
        first, step = groups[0], groups[1] - groups[0]
        some = blocks.reshape(blocks.shape[0], count, group, *blocks.shape[2:])
        some = some[:, first : groups[-1] + 1 : step]
        return some.reshape(blocks.shape[0], len(groups) * group, *blocks.shape[2:])

    received = to_columns(outgoing(blocks, chunks[0]))

    temporal_mix, temporal_back, spatial_mix, spatial_back, *weights, masks = prepare(
        lengths, temporal_weight, spatial_weight, frames, group
    )
    slope, turned = forward(clip, left, right, temporal_mix, spatial_mix, group)
    second = None
    if len(chunks) > 1:
        blocks, spatial_back = lax.optimization_barrier((blocks, spatial_back))
        second = outgoing(blocks, chunks[1])
        second, received = lax.optimization_barrier((second, received))
        second = to_columns(second)
    weights = (slope, turned, masks, *weights)
    deltas, local = [None] * count, None

    def add(received, groups, final):
        some, total = moments(received, *weights, local, groups, group, final)
        for n, delta in zip(groups, some):
            deltas[n] = delta
        return total

    def edge_delta(received, col, place):
        grads = received[:, :, place].transpose(0, 2, 1, 3, 4).reshape(1, frames, rows, chans)
        return (grads.astype(jnp.float32) * slope[col][None]).astype(jnp.bfloat16)

    head = edge_delta(received, 0, 0)
    tail = edge_delta(received, width - 1, received.shape[2] - 1)
    received, head, tail = lax.optimization_barrier((received, head, tail))
    delta_left, delta_right = column_neighbours(head, tail)
    local = add(received, chunks[0], second is None)
    if second is not None:
        local = add(second, chunks[1], True)
    local, deltas, delta_left, delta_right = lax.optimization_barrier(
        (local, deltas, delta_left, delta_right)
    )

    parts = [(0, width), None, None]
    if len(deltas) >= 4:
        half = width // 2
        parts = [(0, half), (half, half), None]

    def one_part(part, state):
        if part is None:
            return state
        operands, filled = state
        return operands, backward(*operands, spatial_back, temporal_back, filled, *part)

    sums, (_, video_grad) = sum_over_devices(
        [half.reshape(-1, chans) for half in local],
        [functools.partial(one_part, part) for part in parts],
        ((deltas, delta_left, delta_right), None),
    )
    low, high = (half.reshape(6, chans, chans) for half in sums)
    temporal_grad = low[:3]
    spatial_grad = jnp.concatenate([low[3:], high]).reshape(3, 3, chans, chans)
    return video_grad[None], temporal_grad, spatial_grad


def solution(mesh):
    placed = (
        P("width", ("tm", "height"), None, None, None),
        P("width", None, "tm", "height", None),
        P(),
        P(),
        P(),
    )
    return jax.shard_map(
        shards,
        mesh=mesh,
        in_specs=placed,
        out_specs=(P("width", ("tm", "height"), None, None, None), P(), P()),
        check_vma=False,
    )
```

```python
import functools

import jax
import jax.numpy as jnp
from jax import lax
from jax.experimental import pallas as pl
from jax.experimental.pallas import tpu as pltpu
from jax.sharding import PartitionSpec as P

MESH_AXES = ("tm", "height", "width")
MIB = 1024 * 1024


def column_neighbours(first, last):
    n_tm, n_height, n_width = (lax.axis_size(axis) for axis in MESH_AXES)
    blocks = n_tm * n_height
    place = [(pos % blocks) * n_width + pos // blocks for pos in range(blocks * n_width)]
    pairs = list(zip(place[:-1], place[1:]))
    left = lax.ppermute(last, MESH_AXES, pairs)
    right = lax.ppermute(first, MESH_AXES, [(b, a) for a, b in pairs])
    return left, right


def prepare_kernel(group, lengths, temporal, spatial, *outs):
    mix, back, pre, grad, temporal_turned, spatial_turned, masks = outs
    frames, chans = masks.shape[1], temporal.shape[1]
    end, spans = jnp.int32(0), []
    for n in range(lengths.shape[0]):
        spans.append((end, end + lengths[n]))
        end = end + lengths[n]
    keep = []
    for frame in range(frames):
        first = jnp.int32(0)
        for start, stop in spans:
            first = first + jnp.where((frame >= start) & (frame < stop), start, 0)
        keep.append([jnp.where(frame - lag >= first, 1.0, 0.0) for lag in range(3)])
    for lag in range(3):
        for frame in range(frames):
            masks[lag, frame] = keep[frame][lag]

    zero = jnp.zeros((chans, chans), jnp.bfloat16)
    turned = [temporal[k].T for k in range(3)]
    for i in range(4):
        for j in range(2):
            at = (slice(i * chans, (i + 1) * chans), slice(j * chans, (j + 1) * chans))
            for p in range(frames // 2):
                k, frame = 2 + j - i, 2 * p + j
                value = zero
                if 0 <= k < 3:
                    value = jnp.where(keep[frame][k] > 0, temporal[k], zero)
                mix[(p, *at)] = value
                k, frame = i - j, 2 * p + i
                value = zero
                if 0 <= k < 3 and frame < frames:
                    value = jnp.where(keep[frame][k] > 0, turned[k], zero)
                back[(p, *at)] = value
    for k in range(3):
        temporal_turned[:, k * chans : (k + 1) * chans] = turned[k]
    for a in range(3):
        for b in range(3):
            value = spatial[a, b].T
            n = 3 * a + b
            spatial_turned[n * chans : (n + 1) * chans] = value
            for j in range(group):
                at = slice(j * chans, (j + 1) * chans)
                i = 3 * (b + j) + a
                pre[i * chans : (i + 1) * chans, at] = spatial[a, b]
                i = 3 * (j + 2 - b) + a
                grad[i * chans : (i + 1) * chans, at] = value
    for j in range(group):
        for i in range(group + 2):
            if not 0 <= i - j < 3:
                at = (slice(3 * i * chans, 3 * (i + 1) * chans), slice(j * chans, (j + 1) * chans))
                pre[at] = jnp.zeros((3 * chans, chans), jnp.bfloat16)
                grad[at] = jnp.zeros((3 * chans, chans), jnp.bfloat16)


def prepare(lengths, temporal, spatial, frames, group):
    chans = temporal.shape[1]

    def wide(*shape):
        return jax.ShapeDtypeStruct(shape, jnp.bfloat16)

    vmem, smem = pl.BlockSpec(memory_space=pltpu.VMEM), pl.BlockSpec(memory_space=pltpu.SMEM)
    return pl.pallas_call(
        functools.partial(prepare_kernel, group),
        in_specs=[smem, vmem, vmem],
        out_specs=[vmem] * 6 + [smem],
        out_shape=[
            wide(frames // 2, 4 * chans, 2 * chans),
            wide(frames // 2, 4 * chans, 2 * chans),
            wide(3 * (group + 2) * chans, group * chans),
            wide(3 * (group + 2) * chans, group * chans),
            wide(chans, 3 * chans),
            wide(9 * chans, chans),
            jax.ShapeDtypeStruct((3, frames), jnp.float32),
        ],
        compiler_params=pltpu.CompilerParams(vmem_limit_bytes=24 * MIB),
        cost_estimate=pl.CostEstimate(flops=0, bytes_accessed=4 << 20, transcendentals=0),
    )(lengths, temporal, spatial)


def row_shifts(block, rows):
    index = lax.broadcasted_iota(jnp.int32, block.shape, 0)
    above = jnp.where(index == 0, 0.0, pltpu.roll(block, 1, 0))
    below = jnp.where(index == rows - 1, 0.0, pltpu.roll(block, rows - 1, 0))
    return above.astype(jnp.bfloat16), below.astype(jnp.bfloat16)


def lanes(parts):
    return parts[0] if len(parts) == 1 else jnp.concatenate(parts, axis=1)


def forward_kernel(group, now, before, left, left_before, right, right_before, *refs):
    temporal, spatial, slope, turned = refs
    width, rows, chans = slope.shape[0], slope.shape[2], slope.shape[3]
    columns = [(left_before.at[0], left.at[0])]
    columns += [(before.at[c], now.at[c]) for c in range(width)]
    columns += [(right_before.at[0], right.at[0])]
    triples = []
    for base in range(0, width + 2, group):
        sources = []
        for e in range(group):
            older, newer = columns[base + e]
            for frame in range(2):
                turned[base + e, frame] = newer[frame].T
            sources.append(lanes([ref[frame] for ref in (older, newer) for frame in range(2)]))
        mixed = jnp.dot(
            jnp.concatenate(sources, axis=0), temporal[0], preferred_element_type=jnp.float32
        ).astype(jnp.bfloat16)
        for e in range(group):
            lines = []
            for frame in range(2):
                value = mixed[e * rows : (e + 1) * rows, frame * chans : (frame + 1) * chans]
                above, below = row_shifts(value.astype(jnp.float32), rows)
                lines.append(lanes([above, value, below]))
            triples.append(jnp.concatenate(lines, axis=0))
    for base in range(0, width, group):
        source = lanes(triples[base : base + group + 2])
        pre = jnp.dot(source, spatial[...], preferred_element_type=jnp.float32)
        sig = jax.nn.sigmoid(pre)
        value = sig * (1.0 + pre * (1.0 - sig))
        for e in range(group):
            slope[base + e] = value[:, e * chans : (e + 1) * chans].reshape(2, rows, chans)


def forward(video, left, right, temporal, spatial, group):
    width, frames, rows, chans = video.shape

    def pair(cols, back):
        return pl.BlockSpec((cols, 2, rows, chans), lambda p: (0, jnp.maximum(p - back, 0), 0, 0))

    pixels = width * frames * rows
    return pl.pallas_call(
        functools.partial(forward_kernel, group),
        grid=(frames // 2,),
        in_specs=[
            pair(width, 0),
            pair(width, 1),
            pair(1, 0),
            pair(1, 1),
            pair(1, 0),
            pair(1, 1),
            pl.BlockSpec((1, 4 * chans, 2 * chans), lambda p: (p, 0, 0)),
            pl.BlockSpec(spatial.shape, lambda p: (0, 0)),
        ],
        out_specs=[
            pair(width, 0),
            pl.BlockSpec((width + 2, 2, chans, rows), lambda p: (0, p, 0, 0)),
        ],
        out_shape=[
            jax.ShapeDtypeStruct((width, frames, rows, chans), jnp.float32),
            jax.ShapeDtypeStruct((width + 2, frames, chans, rows), jnp.bfloat16),
        ],
        compiler_params=pltpu.CompilerParams(vmem_limit_bytes=60 * MIB),
        cost_estimate=pl.CostEstimate(
            flops=pixels * chans * chans * 2 * 24 * 5,
            bytes_accessed=pixels * chans * 14,
            transcendentals=pixels * chans,
        ),
    )(video, video, left, left, right, right, temporal, spatial)


def moments_kernel(group, groups, places, fresh, final, scale, masks, side, *refs):
    count = len(groups)
    grads, refs = refs[0], refs[1:]
    slopes, refs = refs[:count], refs[count:]
    now, before, refs = refs[: len(places)], refs[len(places) : 2 * len(places)], refs[2 * len(places) :]
    temporal, spatial, refs = refs[0], refs[1], refs[2:]
    total, ordered, refs = refs[-2], refs[-1], refs[:-2]
    earlier, refs = (None, refs) if fresh else (refs[0], refs[1:])
    deltas, sums = refs[:count], ordered if final else refs[count]
    pair = pl.program_id(0)
    bands, band = grads.shape[1], grads.shape[4]
    rows, chans = slopes[0].shape[2], slopes[0].shape[3]

    @pl.when(pair == 0)
    def _():
        total[...] = jnp.zeros_like(total)

    parts = [(n, frame) for frame in range(2) for n in range(count)]
    triples = []
    for n, frame in parts:
        line = []
        for e in range(group):
            for b in range(bands):
                at = slice(b * band, (b + 1) * band)
                value = grads[0, b, n * group + e, frame].astype(jnp.float32)
                deltas[n][e, frame, at] = (value * slopes[n][e, frame, at]).astype(jnp.bfloat16)
            value = deltas[n][e, frame]
            above, below = row_shifts(value.astype(jnp.float32), rows)
            line += [below, value, above]
        triples.append(lanes(line))
    right = jnp.concatenate(triples, axis=0)

    def add(lag, left, right):
        total[lag] += jnp.dot(left, right, preferred_element_type=jnp.float32)

    def turned(refs, n, frame):
        first = groups[n] * group
        return jnp.concatenate(
            [
                refs[places.index(c // group)][c % group, frame]
                for c in range(first, first + group + 2)
            ],
            axis=0,
        )

    add(0, lanes([turned(now, n, frame) for n, frame in parts]), right)
    rest = count * rows
    for lag, frame, source, other in (
        (1, 0, before, 1),
        (1, 1, now, 0),
        (2, 0, before, 0),
        (2, 1, before, 1),
    ):

        @pl.when(masks[lag, 2 * pair + frame] > 0)
        def _():
            left = lanes([turned(source, n, other) for n in range(count)])
            add(lag, left, right[frame * rest : (frame + 1) * rest])

    @pl.when(pair == pl.num_programs(0) - 1)
    def _():
        lines = []
        for lag in range(3):
            line = []
            for a in range(3):
                for b in range(3):
                    line.append(
                        sum(
                            total[
                                lag,
                                (j + b) * chans : (j + b + 1) * chans,
                                (j * 3 + a) * chans : (j * 3 + a + 1) * chans,
                            ]
                            for j in range(group)
                        )
                    )
            lines.append(lanes(line))
        moments = jnp.concatenate(lines, axis=0)
        high = moments.astype(jnp.bfloat16)
        low = (moments - high.astype(jnp.float32)).astype(jnp.bfloat16)

        def product(left, right):
            return jnp.dot(left, right, preferred_element_type=jnp.float32)

        spatial_sum = product(temporal[...], high) + product(temporal[...], low)
        temporal_sum = product(high, spatial[...]) + product(low, spatial[...])
        for k in range(3):
            value = temporal_sum[k * chans : (k + 1) * chans] * scale
            sums[k] = value if earlier is None else earlier[k] + value
        for k in range(9):
            value = spatial_sum[:, k * chans : (k + 1) * chans] * scale
            sums[3 + k] = value if earlier is None else earlier[3 + k] + value
        if final:
            half = ordered.shape[0] // 2
            refs[count][...] = ordered[pl.ds(half * side[0], half)]
            refs[count + 1][...] = ordered[pl.ds(half * (1 - side[0]), half)]


def moments(received, slope, turned, masks, temporal, spatial, earlier, groups, group, final):
    fresh = earlier is None
    frames, rows, chans = slope.shape[1:]
    bands, band = received.shape[1], received.shape[4]
    count = len(groups)
    places = sorted({n + k for n in groups for k in range(2 // group + 1)})
    pixels = count * group * frames * rows
    scale = float(frames * rows * slope.shape[0] * lax.axis_size(MESH_AXES)) ** (-0.5)

    def own(n):
        return pl.BlockSpec((group, 2, rows, chans), lambda p, *m: (n, p, 0, 0))

    def columns(n, back):
        return pl.BlockSpec(
            (group, 2, chans, rows), lambda p, *m: (n, jnp.maximum(p - back, 0), 0, 0)
        )

    def whole(shape):
        return pl.BlockSpec(shape, lambda p, *m: (0,) * len(shape))

    sums_shape = (12, chans, chans)
    outs = [(6, chans, chans)] * 2 if final else [sums_shape]
    side = lax.axis_index("width").astype(jnp.int32).reshape(1)
    results = pl.pallas_call(
        functools.partial(moments_kernel, group, groups, places, fresh, final, scale),
        grid_spec=pltpu.PrefetchScalarGridSpec(
            num_scalar_prefetch=2,
            grid=(frames // 2,),
            in_specs=[
                pl.BlockSpec(
                    (1, bands, count * group, 2, band, chans), lambda p, *m: (p, 0, 0, 0, 0, 0)
                )
            ]
            + [own(n) for n in groups]
            + [columns(n, 0) for n in places]
            + [columns(n, 1) for n in places]
            + [whole(temporal.shape), whole(spatial.shape)]
            + ([] if fresh else [whole(sums_shape)]),
            out_specs=[own(0) for _ in groups] + [whole(shape) for shape in outs],
            scratch_shapes=[
                pltpu.VMEM((3, (group + 2) * chans, group * 3 * chans), jnp.float32),
                pltpu.VMEM(sums_shape, jnp.float32),
            ],
        ),
        out_shape=[jax.ShapeDtypeStruct((group, frames, rows, chans), jnp.bfloat16)] * count
        + [jax.ShapeDtypeStruct(shape, jnp.float32) for shape in outs],
        compiler_params=pltpu.CompilerParams(vmem_limit_bytes=60 * MIB),
        cost_estimate=pl.CostEstimate(
            flops=pixels * chans * chans * 2 * 30,
            bytes_accessed=pixels * chans * 20,
            transcendentals=0,
        ),
    )(
        masks,
        side,
        received,
        *([slope] * count),
        *([turned] * (2 * len(places))),
        temporal,
        spatial,
        *([] if fresh else [earlier]),
    )
    return results[:count], results[count:] if final else results[count]


def backward_kernel(group, sources, *refs):
    spatial, temporal = refs[len(sources) : len(sources) + 2]
    out, later = refs[-2:]
    cols, rows, chans = out.shape[0], out.shape[2], out.shape[3]

    @pl.when(pl.program_id(0) == 0)
    def _():
        later[...] = jnp.zeros_like(later)

    triples = []
    for ref, col in zip(refs, sources):
        lines = []
        for frame in range(2):
            value = ref[col, frame]
            above, below = row_shifts(value.astype(jnp.float32), rows)
            lines.append(lanes([below, value, above]))
        triples.append(jnp.concatenate(lines, axis=0))
    grad = []
    for base in range(0, cols, group):
        source = lanes(triples[base : base + group + 2])
        back = jnp.dot(source, spatial[...], preferred_element_type=jnp.float32)
        back = back.astype(jnp.bfloat16)
        for e in range(group):
            at = slice(e * chans, (e + 1) * chans)
            grad.append(lanes([back[f * rows : (f + 1) * rows, at] for f in range(2)]))
    grad = jnp.concatenate(grad, axis=0)
    value = jnp.dot(
        lanes([grad, later[...]]), temporal[0], preferred_element_type=jnp.float32
    ).astype(jnp.bfloat16)
    later[...] = grad
    for col in range(cols):
        for frame in range(2):
            out[col, frame] = value[
                col * rows : (col + 1) * rows, frame * chans : (frame + 1) * chans
            ]


def backward(deltas, left, right, spatial, temporal, filled, first, cols):
    group, frames, rows, chans = deltas[0].shape
    width = group * len(deltas)
    filled = [] if filled is None else [filled]
    ext = [(left, 0)] + [(d, e) for d in deltas for e in range(group)] + [(right, 0)]
    ext = ext[first : first + cols + 2]
    part = first // cols
    last = frames // 2 - 1
    pixels = cols * frames * rows
    block = pl.BlockSpec((cols, 2, rows, chans), lambda p: (part, last - p, 0, 0))
    return pl.pallas_call(
        functools.partial(backward_kernel, group, [0] * len(ext)),
        grid=(frames // 2,),
        in_specs=[
            pl.BlockSpec(
                (1, 2, rows, chans), functools.partial(lambda e, p: (e, last - p, 0, 0), e)
            )
            for _, e in ext
        ]
        + [
            pl.BlockSpec(spatial.shape, lambda p: (0, 0)),
            pl.BlockSpec((1, 4 * chans, 2 * chans), lambda p: (last - p, 0, 0)),
        ]
        + [pl.BlockSpec(memory_space=pl.ANY)] * len(filled),
        out_specs=block,
        out_shape=jax.ShapeDtypeStruct((width, frames, rows, chans), jnp.bfloat16),
        input_output_aliases={len(ext) + 2: 0} if filled else {},
        scratch_shapes=[pltpu.VMEM((cols * rows, 2 * chans), jnp.bfloat16)],
        compiler_params=pltpu.CompilerParams(vmem_limit_bytes=60 * MIB),
        cost_estimate=pl.CostEstimate(
            flops=pixels * chans * chans * 2 * 24,
            bytes_accessed=pixels * chans * 6,
            transcendentals=0,
        ),
    )(*[array for array, _ in ext], spatial, temporal, *filled)


def exchanged(axis, parts):
    count = lax.axis_size(axis)
    return [
        lax.ppermute(parts(s), axis, [(i, i ^ s) for i in range(count)]) for s in range(1, count)
    ]


def sum_over_devices(local, works, state):
    def pieces(value, axis):
        me = lax.axis_index(axis)
        blocks = value.reshape(lax.axis_size(axis), -1, value.shape[-1])
        return lambda s: lax.dynamic_index_in_dim(blocks, me ^ s, 0, keepdims=False)

    def spread(parts, axis):
        order = jnp.arange(len(parts), dtype=jnp.int32) ^ lax.axis_index(axis)
        return jnp.take(jnp.stack(parts), order, axis=0).reshape(-1, parts[0].shape[-1])

    def beside(value, got, work, state):
        value, state = lax.optimization_barrier((value, state))
        got = got(value)
        state = work(state)
        got, state = lax.optimization_barrier((got, state))
        return value, got, state

    keep, send = local
    value = keep + exchanged("width", lambda s: send)[0]
    value, got, state = beside(
        value, lambda v: exchanged("height", pieces(v, "height")), works[0], state
    )
    value = functools.reduce(jnp.add, got, pieces(value, "height")(0))
    value, got, state = beside(value, lambda v: exchanged("tm", lambda s: v), works[1], state)
    value = functools.reduce(jnp.add, got, value)
    value, got, state = beside(value, lambda v: exchanged("height", lambda s: v), works[2], state)
    value = spread([value] + got, "height")
    (other,) = exchanged("width", lambda s: value)
    swap = lax.axis_index("width") == 1
    return [jnp.where(swap, other, value), jnp.where(swap, value, other)], state


def shards(video, out_grad, lengths, temporal_weight, spatial_weight):
    clip = video[0]
    width, frames, rows, chans = clip.shape
    n_tm = lax.axis_size("tm")
    n_height = lax.axis_size("height")
    frames_dev, rows_dev = out_grad.shape[2], out_grad.shape[3]
    assert frames_dev == 2
    group = 2 if width % 2 == 0 else 1
    pairs = frames // 2

    left, right = column_neighbours(clip[:1], clip[width - 1 :])
    blocks = out_grad[0].reshape(n_tm * n_height, width, frames_dev, rows_dev, chans)

    def to_columns(part):
        got = lax.all_to_all(part, ("tm", "height"), split_axis=0, concat_axis=0, tiled=True)
        return got.reshape(n_tm, n_height, *part.shape[1:])

    count = width // group
    chunks = [list(range(count))]
    if count >= 4:
        chunks = [[0, count - 1], list(range(1, count - 1))]

    def outgoing(blocks, groups):
        if len(groups) == count:
            return blocks
        first, step = groups[0], groups[1] - groups[0]
        some = blocks.reshape(blocks.shape[0], count, group, *blocks.shape[2:])
        some = some[:, first : groups[-1] + 1 : step]
        return some.reshape(blocks.shape[0], len(groups) * group, *blocks.shape[2:])

    received = to_columns(outgoing(blocks, chunks[0]))

    temporal_mix, temporal_back, spatial_mix, spatial_back, *weights, masks = prepare(
        lengths, temporal_weight, spatial_weight, frames, group
    )
    slope, turned = forward(clip, left, right, temporal_mix, spatial_mix, group)
    second = None
    if len(chunks) > 1:
        blocks, spatial_back = lax.optimization_barrier((blocks, spatial_back))
        second = outgoing(blocks, chunks[1])
        second, received = lax.optimization_barrier((second, received))
        second = to_columns(second)
    weights = (slope, turned, masks, *weights)
    deltas, local = [None] * count, None

    def add(received, groups, final):
        some, total = moments(received, *weights, local, groups, group, final)
        for n, delta in zip(groups, some):
            deltas[n] = delta
        return total

    def edge_delta(received, col, place):
        grads = received[:, :, place].transpose(0, 2, 1, 3, 4).reshape(1, frames, rows, chans)
        return (grads.astype(jnp.float32) * slope[col][None]).astype(jnp.bfloat16)

    head = edge_delta(received, 0, 0)
    tail = edge_delta(received, width - 1, received.shape[2] - 1)
    local = add(received, chunks[0], second is None)
    local, head, tail = lax.optimization_barrier((local, head, tail))
    delta_left, delta_right = column_neighbours(head, tail)
    if second is not None:
        local = add(second, chunks[1], True)
    local, deltas, delta_left, delta_right = lax.optimization_barrier(
        (local, deltas, delta_left, delta_right)
    )

    parts = [(0, width), None, None]
    if len(deltas) >= 4:
        half = width // 2
        parts = [(0, half), (half, half), None]

    def one_part(part, state):
        if part is None:
            return state
        operands, filled = state
        return operands, backward(*operands, spatial_back, temporal_back, filled, *part)

    sums, (_, video_grad) = sum_over_devices(
        [half.reshape(-1, chans) for half in local],
        [functools.partial(one_part, part) for part in parts],
        ((deltas, delta_left, delta_right), None),
    )
    low, high = (half.reshape(6, chans, chans) for half in sums)
    temporal_grad = low[:3]
    spatial_grad = jnp.concatenate([low[3:], high]).reshape(3, 3, chans, chans)
    return video_grad[None], temporal_grad, spatial_grad


def solution(mesh):
    placed = (
        P("width", ("tm", "height"), None, None, None),
        P("width", None, "tm", "height", None),
        P(),
        P(),
        P(),
    )
    return jax.shard_map(
        shards,
        mesh=mesh,
        in_specs=placed,
        out_specs=(P("width", ("tm", "height"), None, None, None), P(), P()),
        check_vma=False,
    )
```
